32 devices in a mesh: grp: 4 (over z), dev: 8 (over y, x, core).
Axes of the slice: x: 2, y: 2, z: 4, core: 2. Of those that a mesh axis runs over, the one named last changes fastest.
Arguments:
- series: float32 [2, 4194304], P(None, ('grp', 'dev')), may hold values from -6 to 6
Outputs:
- spectrum: float32 [2, 4194304], P(None, ('grp', 'dev'))
The draws below stay inside these ranges and needn't reach their ends.
All inputs are finite; a program needn't handle non-finite values.
Results may differ from the reference program's by a relative error of at most 0.00007.
Values sent between devices are 32-bit elements; how exact they have to be, the bound alone decides.
No kernel may reach another device: no remote copies, remote signals or barrier semaphores. Data moves between devices by JAX's collectives and lax.ppermute only.
A program may use at most 128 MiB of HBM per device.

```python
import math
import jax
import jax.numpy as jnp

POINTS = 4194304


def steps_of(rng, dims, shards, smallest, largest):
    loudness, own = 1.0, jax.random.fold_in(rng, 6)
    for axis_at, blocks in shards:
        heights = jnp.exp(jax.random.uniform(jax.random.fold_in(own, axis_at), (blocks,), jnp.float32, smallest / len(shards), largest / len(shards)))
        loudness = loudness * jnp.repeat(heights, dims[axis_at] // blocks).reshape([-1 if axis == axis_at else 1 for axis in range(len(dims))])
    return loudness


def bell_draw(rng, extent, scale, reach, shards=(), dtype=jnp.bfloat16):
    level = steps_of(rng, extent, shards, -0.22, 0.18) if shards else 1.0
    array = jax.random.normal(rng, extent, jnp.float32) * scale * level
    return jnp.minimum(jnp.maximum(array, -reach), reach).astype(dtype)


def setup_inputs(seed: int = 0) -> dict:
    splits = jax.random.split(jax.random.key(seed), 2)
    return {
        "series": bell_draw(splits[0], (2, POINTS), 1.0, 6.0, ((1, 32),), jnp.float32),
    }


def reference(series):
    scaled = series * (1.0 / math.sqrt(POINTS))
    signal = scaled[0] + 1j * scaled[1]
    result = jnp.fft.fft(signal)
    return jnp.stack([jnp.real(result), jnp.imag(result)])
```

```python
import functools
import math

import jax
import jax.numpy as jnp
import numpy as np
from jax import lax
from jax.experimental import pallas as pl
from jax.experimental.pallas import tpu as pltpu
from jax.sharding import PartitionSpec as P

LANES = 128
SUB = 8
AXES = ("grp", "dev")
ORDER = ("dev", "grp")


def roots(product, modulus):
    angle = np.asarray(product, np.int64) % modulus * (-2.0 * math.pi / modulus)
    return np.cos(angle), np.sin(angle)


def times_root(value, k, n):
    re, im = value
    k %= n
    if k == 0:
        return value
    if 4 * k == n:
        return im, -re
    if 2 * k == n:
        return -re, -im
    if 4 * k == 3 * n:
        return -im, re
    if 8 * k == n:
        half = np.float32(math.sqrt(0.5))
        return (re + im) * half, (im - re) * half
    if 8 * k == 3 * n:
        half = np.float32(math.sqrt(0.5))
        return (im - re) * half, (re + im) * -half
    angle = -2.0 * math.pi * k / n
    c, s = np.float32(math.cos(angle)), np.float32(math.sin(angle))
    return re * c - im * s, re * s + im * c


def dft_list(values):
    n = len(values)
    if n == 1:
        return values
    even, odd = dft_list(values[0::2]), dft_list(values[1::2])
    low, high = [], []
    for k in range(n // 2):
        (er, ei), (tr, ti) = even[k], times_root(odd[k], k, n)
        low.append((er + tr, ei + ti))
        high.append((er - tr, ei - ti))
    return low + high


def across_kernel(sources, place_ref, turn_ref, step_ref, in_ref, out_ref):
    count = len(sources)
    rows = in_ref.shape[0] // count // 2
    for j in range(0, rows, SUB):
        take = min(SUB, rows - j)
        values = []
        for at in sources:
            base = (at * rows + j) * 2
            values.append((in_ref[pl.ds(base, take, 2), :], in_ref[pl.ds(base + 1, take, 2), :]))
        for k, (re, im) in enumerate(dft_list(values)):
            base = k * 2 * rows + j
            tc, ts = turn_ref[base : base + take, :], turn_ref[base + rows : base + rows + take, :]
            dc, ds = step_ref[0, 2 * k], step_ref[0, 2 * k + 1]
            c, s = tc * dc - ts * ds, tc * ds + ts * dc
            out_ref[base : base + take, :] = re * c - im * s
            out_ref[base + rows : base + rows + take, :] = re * s + im * c


def across(received, sources, points, scale):
    count = len(sources)
    slab = points // count
    piece = slab // count
    digits = np.arange(count)
    tc, ts = roots(digits[:, None] * np.arange(piece)[None, :], points)
    turn = np.stack([tc, ts], 1).reshape(count * 2 * piece // LANES, LANES) * scale
    dc, ds = roots(digits[:, None] * digits[None, :], count * count)
    step = np.stack([dc, ds], 2).reshape(count, 1, 2 * count)
    place = lax.axis_index(ORDER).astype(jnp.int32).reshape(1)
    whole = pl.BlockSpec(received.shape, lambda i, place: (0, 0))
    return pl.pallas_call(
        functools.partial(across_kernel, sources),
        grid_spec=pltpu.PrefetchScalarGridSpec(
            num_scalar_prefetch=1,
            grid=(1,),
            in_specs=[
                whole,
                pl.BlockSpec((None, 1, 2 * count), lambda i, place: (place[0], 0, 0), memory_space=pltpu.SMEM),
                whole,
            ],
            out_specs=whole,
        ),
        out_shape=jax.ShapeDtypeStruct(received.shape, jnp.float32),
        compiler_params=pltpu.CompilerParams(vmem_limit_bytes=32 << 20),
    )(place, turn.astype(np.float32), step.astype(np.float32), received)


def split_bf16(values):
    high = values.astype(jnp.bfloat16)
    return high, (values - high.astype(jnp.float32)).astype(jnp.bfloat16)


def lane_stage(outer, inner, turn_ref, fh_ref, fl_ref, out_ref, first, second):
    span = outer * inner
    fold = outer // SUB
    for v in range(fold):
        values = []
        for j in range(inner):
            base = v * inner + j
            values.append(
                (
                    first[pl.ds(base, SUB, fold * inner), :],
                    first[pl.ds(span + base, SUB, fold * inner), :],
                )
            )
        for k, (re, im) in enumerate(dft_list(values)):
            base = (v * inner + k) * SUB
            c, s = turn_ref[base : base + SUB, :], turn_ref[span + base : span + base + SUB, :]
            second[base : base + SUB, :LANES] = re * c - im * s
            second[base : base + SUB, LANES:] = re * s + im * c
    xh, xl = split_bf16(second[...])
    dot = functools.partial(
        lax.dot_general, dimension_numbers=(((1,), (1,)), ((), ())), preferred_element_type=jnp.float32
    )
    result = dot(fh_ref[...], xh) + (dot(fh_ref[...], xl) + dot(fl_ref[...], xh))
    for t in range(span // LANES):
        tile = result[:, t * LANES : (t + 1) * LANES]
        out_ref[:, t * SUB : (t + 1) * SUB, :] = tile.reshape(tile.shape[0] // SUB, SUB, LANES)


def local_kernel(piece_rows, mid_ref, turn_ref, fh_ref, fl_ref, in_ref, out_ref, first, second):
    inner = piece_rows
    outer = in_ref.shape[0] // 2 // inner
    span = outer * inner
    for j in range(0, inner, SUB):
        take = min(SUB, inner - j)
        values = []
        for e in range(outer):
            base = e * 2 * inner + j
            values.append((in_ref[base : base + take, :], in_ref[base + inner : base + inner + take, :]))
        for k, (re, im) in enumerate(dft_list(values)):
            base = k * inner + j
            c, s = mid_ref[base : base + take, :], mid_ref[span + base : span + base + take, :]
            first[base : base + take, :] = re * c - im * s
            first[span + base : span + base + take, :] = re * s + im * c
    lane_stage(outer, inner, turn_ref, fh_ref, fl_ref, out_ref, first, second)


def local_tables(outer, inner, lane_rows):
    span = outer * inner
    slab = span * LANES
    mc, ms = roots(np.arange(outer)[:, None] * np.arange(inner)[None, :], span)
    mid = np.broadcast_to(np.stack([mc, ms]).reshape(2 * span, 1), (2 * span, LANES))
    fold = outer // SUB
    v, k, i = np.meshgrid(np.arange(fold), np.arange(inner), np.arange(SUB), indexing="ij")
    kept = ((v + fold * i) + outer * k).reshape(span)
    tc, ts = roots(kept[:, None] * np.arange(LANES)[None, :], slab)
    turn = np.concatenate([tc, ts])
    freq, imag = lane_rows
    fc, fs = roots(freq[:, None] * np.arange(LANES)[None, :], LANES)
    lane = np.where(imag[:, None], np.concatenate([fs, fc], 1), np.concatenate([fc, -fs], 1)).astype(np.float32)
    fh = lane.astype(jnp.bfloat16)
    fl = (lane - fh.astype(np.float32)).astype(jnp.bfloat16)
    return mid.astype(np.float32), turn.astype(np.float32), fh, fl, kept


def local_transform(arrived, outer, inner, lane_rows):
    span = outer * inner
    mid, turn, fh, fl, kept = local_tables(outer, inner, lane_rows)
    return pl.pallas_call(
        functools.partial(local_kernel, inner),
        out_shape=jax.ShapeDtypeStruct((2 * LANES // SUB, SUB * span // LANES, LANES), jnp.float32),
        scratch_shapes=[
            pltpu.VMEM((2 * span, LANES), jnp.float32),
            pltpu.VMEM((span, 2 * LANES), jnp.float32),
        ],
        compiler_params=pltpu.CompilerParams(vmem_limit_bytes=48 << 20),
    )(mid, turn, fh, fl, arrived), kept


def order_kernel(sources, in_ref, out_ref, whole):
    count = len(sources)
    fold = LANES // count
    each = in_ref.shape[0] // count
    tiles = each // SUB // fold
    lows = SUB // 2
    for k, at in enumerate(sources):
        whole[k * each : (k + 1) * each, :] = in_ref[at * each : (at + 1) * each, :]
    for c in range(2):
        for low in range(lows):
            for t in range(tiles):
                parts = [
                    whole[pl.ds((v * tiles + t) * SUB + c * lows + low, count, each), :] for v in range(fold)
                ]
                base = (low * tiles + t) * LANES * 2 + c
                out_ref[pl.ds(base, LANES, 2), :] = jnp.concatenate(parts, 0).T


def order_rows(landed, sources):
    return pl.pallas_call(
        functools.partial(order_kernel, sources),
        out_shape=jax.ShapeDtypeStruct(landed.shape, jnp.float32),
        scratch_shapes=[pltpu.VMEM(landed.shape, jnp.float32)],
        compiler_params=pltpu.CompilerParams(vmem_limit_bytes=32 << 20),
    )(landed)


VMEM_WHOLE = pl.BlockSpec(memory_space=pltpu.VMEM)
FAR_FIRST = (0, 2, 3, 1)


def own_place():
    return lax.axis_index("grp") * 8 + lax.axis_index("dev")


def spread(row, at):
    return jnp.broadcast_to(row[:, at : at + 1], (SUB, LANES))


def mix_kernel(woven, coef_ref, *refs):
    ins, outs = [None] * 4, [None] * 4
    for n, m in enumerate(FAR_FIRST):
        ins[m], outs[m] = refs[n], refs[4 + n]
    rows = refs[0].shape[0] // 2
    row = coef_ref[pl.ds(own_place(), 1), :]
    parity = spread(row, 0)
    turns = [(spread(row, 1 + 2 * m), spread(row, 2 + 2 * m)) for m in range(2)]
    blocks = len(woven)
    for b in range(blocks):
        factors = [(spread(row, 5 + 8 * b + 2 * m), spread(row, 6 + 8 * b + 2 * m)) for m in range(4)]
        for r in range(b * rows // blocks, (b + 1) * rows // blocks, SUB):
            if woven[b]:
                values = [(ref[pl.ds(2 * r, SUB, 2), :], ref[pl.ds(2 * r + 1, SUB, 2), :]) for ref in ins]
            else:
                values = [(ref[r : r + SUB, :], ref[rows + r : rows + r + SUB, :]) for ref in ins]
            (r0, i0), (r1, i1), (r2, i2), (r3, i3) = values
            r2, i2, r3, i3 = r2 * parity, i2 * parity, r3 * parity, i3 * parity
            results = [None] * 4
            for m, (pr, pi, qr, qi) in enumerate(
                ((r0 + r2, i0 + i2, r1 + r3, i1 + i3), (r0 - r2, i0 - i2, r1 - r3, i1 - i3))
            ):
                tc, ts = turns[m]
                tr, ti = qr * tc - qi * ts, qr * ts + qi * tc
                results[m], results[m + 2] = (pr + tr, pi + ti), (pr - tr, pi - ti)
            for out, (re, im), (c, s) in zip(outs, results, factors):
                out[r : r + SUB, :] = re * c - im * s
                out[rows + r : rows + r + SUB, :] = re * s + im * c


def mix(parts, woven, table):
    work = sum(part.size for part in parts)
    mixed = pl.pallas_call(
        functools.partial(mix_kernel, woven),
        in_specs=[VMEM_WHOLE] * 5,
        out_shape=[jax.ShapeDtypeStruct(parts[0].shape, jnp.float32)] * 4,
        cost_estimate=pl.CostEstimate(flops=8 * work, bytes_accessed=8 * work, transcendentals=0),
        compiler_params=pltpu.CompilerParams(vmem_limit_bytes=16 << 20),
    )(table, *[parts[m] for m in FAR_FIRST])
    return [mixed[FAR_FIRST.index(m)] for m in range(4)]


def quarter_kernel(start, in_ref, *refs):
    out_refs, sems = refs[:-1], refs[-1]
    quarter = in_ref.shape[1] // len(out_refs)
    group = lax.axis_index("grp")
    copies = []
    for m, out_ref in enumerate(out_refs):
        at = pl.multiple_of((group ^ m) * quarter + start, LANES)
        copies.append(pltpu.make_async_copy(in_ref.at[:, pl.ds(at, out_ref.shape[1])], out_ref, sems.at[m]))
        copies[-1].start()
    for copy in copies:
        copy.wait()


def quarters(series, start, size):
    parts = pl.pallas_call(
        functools.partial(quarter_kernel, start),
        in_specs=[pl.BlockSpec(memory_space=pl.ANY)],
        out_specs=[VMEM_WHOLE] * 4,
        out_shape=[jax.ShapeDtypeStruct((2, size), jnp.float32)] * 4,
        scratch_shapes=[pltpu.SemaphoreType.DMA((4,))],
        compiler_params=pltpu.CompilerParams(vmem_limit_bytes=56 << 20),
    )(series)
    return [part.reshape(2, size // LANES, LANES).transpose(1, 0, 2).reshape(-1, LANES) for part in parts]


def swap(parts, shift):
    return [send(part, m << shift) if m else part for m, part in enumerate(parts)]


def send(part, flip):
    return lax.ppermute(part, AXES, [(d, d ^ flip) for d in range(lax.axis_size(AXES))])


def device_digits():
    d = np.arange(32)
    z, yx, core = d // 8, d // 2 % 4, d % 2
    return z, yx, core, yx + 4 * z + 16 * core


def root(product, modulus):
    c, s = roots(product, modulus)
    return c + 1j * s


def rows_of(columns):
    flat = [columns[0].real] + [part for column in columns[1:] for part in (column.real, column.imag)]
    table = np.zeros((32, LANES), np.float32)
    table[:, : len(flat)] = np.stack(flat, 1)
    return table


def mix_table(mine, digit, factors):
    columns = [root((mine ^ 2) * digit - mine * digit, 4)]
    columns += [root(((mine ^ 1) - mine) * (digit ^ m), 4) for m in range(2)]
    return rows_of(columns + [f * root(mine * (digit ^ m), 4) for block in factors for m, f in enumerate(block)])


def mix_tables(points, start, rows):
    z, yx, core, _ = device_digits()
    first = [[root((2 * yx + core) * (yx ^ m), 32) / math.sqrt(points) for m in range(4)]]
    second = [
        [root(core * (z ^ m), 8) * root((yx + 4 * (z ^ m)) * (z * 8 + start // 32 + b), 1024) for m in range(4)]
        for b in range(rows // 32)
    ]
    return mix_table(z, yx, first), mix_table(yx, z, second)


def slab_kernel(starts, bit_ref, near_ref, mid_ref, turn_ref, fh_ref, fl_ref, *refs):
    in_refs, (out_ref, whole, first, second) = refs[:-4], refs[-4:]
    place = own_place()
    group, pair, core = place // 8, place // 2 % 4, place % 2
    digit = pair + 4 * group + 16 * core
    row = bit_ref[pl.ds(place, 1), :]
    sign = spread(row, 0)
    span, block = 1024, 0
    for h, start in enumerate(starts):
        for m in range(4):
            mine, other = in_refs[h * 8 + FAR_FIRST.index(m)], in_refs[h * 8 + 4 + FAR_FIRST.index(m)]
            rows = mine.shape[0] // 2
            at = pl.multiple_of((group ^ m) * (span // 4) + start, 32)
            for b in range(0, rows, 32):
                c, s = spread(row, 1 + 2 * block), spread(row, 2 + 2 * block)
                block += 1
                for r in range(b, b + 32, SUB):
                    re = other[r : r + SUB, :] + mine[r : r + SUB, :] * sign
                    im = other[rows + r : rows + r + SUB, :] + mine[rows + r : rows + r + SUB, :] * sign
                    whole[pl.ds(at + r, SUB), :] = re * c - im * s
                    whole[pl.ds(span + at + r, SUB), :] = re * s + im * c
    outer = inner = 32
    for j in range(0, inner, SUB):
        values = []
        for e in range(outer):
            base = e * inner + j
            values.append((whole[base : base + SUB, :], whole[span + base : span + base + SUB, :]))
        at = pl.multiple_of(digit * 2 * inner + j, SUB)
        nc, ns = near_ref[pl.ds(at, SUB), :], near_ref[pl.ds(at + inner, SUB), :]
        for k, (re, im) in enumerate(dft_list(values)):
            base = k * inner + j
            mc, ms = mid_ref[base : base + SUB, :], mid_ref[span + base : span + base + SUB, :]
            c, s = mc * nc - ms * ns, mc * ns + ms * nc
            first[base : base + SUB, :] = re * c - im * s
            first[span + base : span + base + SUB, :] = re * s + im * c
    lane_stage(outer, inner, turn_ref, fh_ref, fl_ref, out_ref, first, second)


def slab_transform(arrived, lane_rows, points):
    z, _, core, _ = device_digits()
    nc, ns = roots(np.arange(32)[:, None] * np.arange(32 * LANES)[None, :], points)
    near = np.stack([nc, ns], 1).reshape(32 * 2 * 32, LANES).astype(np.float32)
    mid, turn, fh, fl, _ = local_tables(32, 32, lane_rows)
    starts = [sum(CHUNKS[:h]) for h in range(len(CHUNKS))]
    bits = [1 - 2 * core + 0j]
    for start, rows in zip(starts, CHUNKS):
        for m in range(4):
            bits += [root(core * ((z ^ m) * 8 + start // 32 + b), 64) for b in range(rows // 32)]
    return pl.pallas_call(
        functools.partial(slab_kernel, starts),
        in_specs=[VMEM_WHOLE] * (6 + len(arrived)),
        out_shape=jax.ShapeDtypeStruct((32, 64, LANES), jnp.float32),
        scratch_shapes=[
            pltpu.VMEM((2048, LANES), jnp.float32),
            pltpu.VMEM((2048, LANES), jnp.float32),
            pltpu.VMEM((1024, 2 * LANES), jnp.float32),
        ],
        compiler_params=pltpu.CompilerParams(vmem_limit_bytes=48 << 20),
    )(rows_of(bits), near, mid, turn, fh, fl, *arrived)


CHUNKS = (128, 128)


def by_axes(series, points):
    slab = series.shape[1]
    arrived = []
    for h, rows in enumerate(CHUNKS):
        start = sum(CHUNKS[:h])
        first, second = mix_tables(points, start, rows)
        parts = swap(quarters(series, start * LANES, rows * LANES), 3)
        parts = swap(mix(parts, (True,), first), 1)
        parts = swap(mix(parts, (False,) * (rows // 32), second), 3)
        mine = [parts[m] for m in FAR_FIRST]
        arrived += mine + [send(part, 1) for part in mine]
    dest, c, low = np.meshgrid(np.arange(32), np.arange(2), np.arange(4), indexing="ij")
    lane_rows = ((dest * 4 + low).reshape(-1), (c == 1).reshape(-1))
    spectrum = slab_transform(arrived, lane_rows, points)
    landed = lax.all_to_all(spectrum, AXES, split_axis=0, concat_axis=0, tiled=True).reshape(2048, LANES)
    ordered = order_rows(landed, np.argsort(device_digits()[3]).tolist())
    return ordered.reshape(slab // LANES, 2, LANES).transpose(1, 0, 2).reshape(2, slab)


def exchange(blocks, count):
    shape = blocks.shape
    blocks = blocks.reshape((count, shape[0] // count) + shape[1:])
    return lax.all_to_all(blocks, ORDER, split_axis=0, concat_axis=0, tiled=True).reshape(shape)


def local(series):
    count = lax.axis_size("grp") * lax.axis_size("dev")
    slab = series.shape[1]
    points = slab * count
    piece_rows = slab // count // LANES
    if (lax.axis_size("grp"), lax.axis_size("dev"), slab) == (4, 8, 1024 * LANES):
        return by_axes(series, points)
    at = np.arange(count).reshape(lax.axis_size("dev"), lax.axis_size("grp")).T.reshape(-1)
    owners = np.argsort(at)
    tiles = series.reshape(2, count, piece_rows, LANES).transpose(1, 2, 0, 3)
    received = exchange(tiles, count).reshape(2 * slab // LANES, LANES)
    turned = across(received, at.tolist(), points, 1.0 / math.sqrt(points))
    arrived = exchange(turned, count)
    if 2 * LANES == SUB * count:
        lows = LANES // count
        dest, c, low = np.meshgrid(owners, np.arange(2), np.arange(lows), indexing="ij")
        lane_rows = ((dest * lows + low).reshape(-1), (c == 1).reshape(-1))
        spectrum, _ = local_transform(arrived, count, piece_rows, lane_rows)
        landed = exchange(spectrum.reshape(turned.shape), count)
        ordered = order_rows(landed, list(range(count)))
        return ordered.reshape(slab // LANES, 2, LANES).transpose(1, 0, 2).reshape(2, slab)
    freq, c = np.meshgrid(np.arange(LANES), np.arange(2), indexing="ij")
    spectrum, kept = local_transform(arrived, count, piece_rows, (freq.reshape(-1), (c == 1).reshape(-1)))
    spectrum = spectrum.reshape(2 * LANES // SUB, -1, SUB, LANES).transpose(0, 2, 1, 3).reshape(2 * LANES, -1)
    natural = jnp.take(spectrum, np.argsort(kept), axis=1).reshape(LANES, 2, -1)
    blocks = natural.transpose(0, 2, 1).reshape(count, -1, 2)[owners]
    landed = exchange(blocks, count)
    return landed.transpose(2, 1, 0).reshape(2, slab)


def solution(mesh):
    return jax.shard_map(
        local,
        mesh=mesh,
        in_specs=(P(None, AXES),),
        out_specs=P(None, AXES),
        check_vma=False,
    )
```

```python
import functools
import math

import jax
import jax.numpy as jnp
import numpy as np
from jax import lax
from jax.experimental import pallas as pl
from jax.experimental.pallas import tpu as pltpu
from jax.sharding import PartitionSpec as P

LANES = 128
SUB = 8
AXES = ("grp", "dev")
ORDER = ("dev", "grp")


def roots(product, modulus):
    angle = np.asarray(product, np.int64) % modulus * (-2.0 * math.pi / modulus)
    return np.cos(angle), np.sin(angle)


def times_root(value, k, n):
    re, im = value
    k %= n
    if k == 0:
        return value
    if 4 * k == n:
        return im, -re
    if 2 * k == n:
        return -re, -im
    if 4 * k == 3 * n:
        return -im, re
    if 8 * k == n:
        half = np.float32(math.sqrt(0.5))
        return (re + im) * half, (im - re) * half
    if 8 * k == 3 * n:
        half = np.float32(math.sqrt(0.5))
        return (im - re) * half, (re + im) * -half
    angle = -2.0 * math.pi * k / n
    c, s = np.float32(math.cos(angle)), np.float32(math.sin(angle))
    return re * c - im * s, re * s + im * c


def dft_list(values):
    n = len(values)
    if n == 1:
        return values
    even, odd = dft_list(values[0::2]), dft_list(values[1::2])
    low, high = [], []
    for k in range(n // 2):
        (er, ei), (tr, ti) = even[k], times_root(odd[k], k, n)
        low.append((er + tr, ei + ti))
        high.append((er - tr, ei - ti))
    return low + high


def across_kernel(sources, place_ref, turn_ref, step_ref, in_ref, out_ref):
    count = len(sources)
    rows = in_ref.shape[0] // count // 2
    for j in range(0, rows, SUB):
        take = min(SUB, rows - j)
        values = []
        for at in sources:
            base = (at * rows + j) * 2
            values.append((in_ref[pl.ds(base, take, 2), :], in_ref[pl.ds(base + 1, take, 2), :]))
        for k, (re, im) in enumerate(dft_list(values)):
            base = k * 2 * rows + j
            tc, ts = turn_ref[base : base + take, :], turn_ref[base + rows : base + rows + take, :]
            dc, ds = step_ref[0, 2 * k], step_ref[0, 2 * k + 1]
            c, s = tc * dc - ts * ds, tc * ds + ts * dc
            out_ref[base : base + take, :] = re * c - im * s
            out_ref[base + rows : base + rows + take, :] = re * s + im * c


def across(received, sources, points, scale):
    count = len(sources)
    slab = points // count
    piece = slab // count
    digits = np.arange(count)
    tc, ts = roots(digits[:, None] * np.arange(piece)[None, :], points)
    turn = np.stack([tc, ts], 1).reshape(count * 2 * piece // LANES, LANES) * scale
    dc, ds = roots(digits[:, None] * digits[None, :], count * count)
    step = np.stack([dc, ds], 2).reshape(count, 1, 2 * count)
    place = lax.axis_index(ORDER).astype(jnp.int32).reshape(1)
    whole = pl.BlockSpec(received.shape, lambda i, place: (0, 0))
    return pl.pallas_call(
        functools.partial(across_kernel, sources),
        grid_spec=pltpu.PrefetchScalarGridSpec(
            num_scalar_prefetch=1,
            grid=(1,),
            in_specs=[
                whole,
                pl.BlockSpec((None, 1, 2 * count), lambda i, place: (place[0], 0, 0), memory_space=pltpu.SMEM),
                whole,
            ],
            out_specs=whole,
        ),
        out_shape=jax.ShapeDtypeStruct(received.shape, jnp.float32),
        compiler_params=pltpu.CompilerParams(vmem_limit_bytes=32 << 20),
    )(place, turn.astype(np.float32), step.astype(np.float32), received)


def split_bf16(values):
    high = values.astype(jnp.bfloat16)
    return high, (values - high.astype(jnp.float32)).astype(jnp.bfloat16)


def lane_stage(outer, inner, turn_ref, fh_ref, fl_ref, out_ref, first, second):
    span = outer * inner
    fold = outer // SUB
    together = max(1, LANES // (inner * SUB))
    dot = functools.partial(
        lax.dot_general, dimension_numbers=(((1,), (1,)), ((), ())), preferred_element_type=jnp.float32
    )
    for begin in range(0, fold, together):
        for v in range(begin, begin + together):
            values = []
            for j in range(inner):
                base = v * inner + j
                values.append(
                    (
                        first[pl.ds(base, SUB, fold * inner), :],
                        first[pl.ds(span + base, SUB, fold * inner), :],
                    )
                )
            for k, (re, im) in enumerate(dft_list(values)):
                base = (v * inner + k) * SUB
                c, s = turn_ref[base : base + SUB, :], turn_ref[span + base : span + base + SUB, :]
                second[base : base + SUB, :LANES] = re * c - im * s
                second[base : base + SUB, LANES:] = re * s + im * c
        columns = together * inner * SUB
        done = begin * inner * SUB
        xh, xl = split_bf16(second[done : done + columns, :])
        result = dot(fh_ref[...], xh) + (dot(fh_ref[...], xl) + dot(fl_ref[...], xh))
        for t in range(columns // LANES):
            tile = result[:, t * LANES : (t + 1) * LANES]
            at = (done // LANES + t) * SUB
            out_ref[:, at : at + SUB, :] = tile.reshape(tile.shape[0] // SUB, SUB, LANES)


def local_kernel(piece_rows, mid_ref, turn_ref, fh_ref, fl_ref, in_ref, out_ref, first, second):
    inner = piece_rows
    outer = in_ref.shape[0] // 2 // inner
    span = outer * inner
    for j in range(0, inner, SUB):
        take = min(SUB, inner - j)
        values = []
        for e in range(outer):
            base = e * 2 * inner + j
            values.append((in_ref[base : base + take, :], in_ref[base + inner : base + inner + take, :]))
        for k, (re, im) in enumerate(dft_list(values)):
            base = k * inner + j
            c, s = mid_ref[base : base + take, :], mid_ref[span + base : span + base + take, :]
            first[base : base + take, :] = re * c - im * s
            first[span + base : span + base + take, :] = re * s + im * c
    lane_stage(outer, inner, turn_ref, fh_ref, fl_ref, out_ref, first, second)


def local_tables(outer, inner, lane_rows):
    span = outer * inner
    slab = span * LANES
    mc, ms = roots(np.arange(outer)[:, None] * np.arange(inner)[None, :], span)
    mid = np.broadcast_to(np.stack([mc, ms]).reshape(2 * span, 1), (2 * span, LANES))
    fold = outer // SUB
    v, k, i = np.meshgrid(np.arange(fold), np.arange(inner), np.arange(SUB), indexing="ij")
    kept = ((v + fold * i) + outer * k).reshape(span)
    tc, ts = roots(kept[:, None] * np.arange(LANES)[None, :], slab)
    turn = np.concatenate([tc, ts])
    freq, imag = lane_rows
    fc, fs = roots(freq[:, None] * np.arange(LANES)[None, :], LANES)
    lane = np.where(imag[:, None], np.concatenate([fs, fc], 1), np.concatenate([fc, -fs], 1)).astype(np.float32)
    fh = lane.astype(jnp.bfloat16)
    fl = (lane - fh.astype(np.float32)).astype(jnp.bfloat16)
    return mid.astype(np.float32), turn.astype(np.float32), fh, fl, kept


def local_transform(arrived, outer, inner, lane_rows):
    span = outer * inner
    mid, turn, fh, fl, kept = local_tables(outer, inner, lane_rows)
    return pl.pallas_call(
        functools.partial(local_kernel, inner),
        out_shape=jax.ShapeDtypeStruct((2 * LANES // SUB, SUB * span // LANES, LANES), jnp.float32),
        scratch_shapes=[
            pltpu.VMEM((2 * span, LANES), jnp.float32),
            pltpu.VMEM((span, 2 * LANES), jnp.float32),
        ],
        compiler_params=pltpu.CompilerParams(vmem_limit_bytes=20 << 20),
    )(mid, turn, fh, fl, arrived), kept


def order_kernel(sources, in_ref, out_ref, whole, ordered, sems):
    count = len(sources)
    fold = LANES // count
    each = in_ref.shape[0] // count
    tiles = each // SUB // fold
    lows = SUB // 2
    rows = tiles * LANES * 2
    for k, at in enumerate(sources):
        whole[k * each : (k + 1) * each, :] = in_ref[at * each : (at + 1) * each, :]
    copies = []
    for low in range(lows):
        for c in range(2):
            for t in range(tiles):
                parts = [
                    whole[pl.ds((v * tiles + t) * SUB + c * lows + low, count, each), :] for v in range(fold)
                ]
                ordered[pl.ds(low * rows + t * LANES * 2 + c, LANES, 2), :] = jnp.concatenate(parts, 0).T
        piece = pl.ds(low * rows, rows)
        copies.append(pltpu.make_async_copy(ordered.at[piece, :], out_ref.at[piece, :], sems.at[low]))
        copies[-1].start()
    for copy in copies:
        copy.wait()


def order_rows(landed, sources):
    return pl.pallas_call(
        functools.partial(order_kernel, sources),
        in_specs=[pl.BlockSpec(memory_space=pltpu.VMEM)],
        out_specs=pl.BlockSpec(memory_space=pltpu.HBM),
        out_shape=jax.ShapeDtypeStruct(landed.shape, jnp.float32),
        scratch_shapes=[
            pltpu.VMEM(landed.shape, jnp.float32),
            pltpu.VMEM(landed.shape, jnp.float32),
            pltpu.SemaphoreType.DMA((SUB // 2,)),
        ],
        compiler_params=pltpu.CompilerParams(vmem_limit_bytes=16 << 20),
    )(landed)


VMEM_WHOLE = pl.BlockSpec(memory_space=pltpu.VMEM)
FAR_FIRST = (0, 2, 3, 1)


def own_place():
    return lax.axis_index("grp") * 8 + lax.axis_index("dev")


def spread(row, at):
    return jnp.broadcast_to(row[:, at : at + 1], (SUB, LANES))


def mix_kernel(woven, coef_ref, *refs):
    ins, outs = [None] * 4, [None] * 4
    for n, m in enumerate(FAR_FIRST):
        ins[m], outs[m] = refs[n], refs[4 + n]
    rows = refs[0].shape[0] // 2
    row = coef_ref[pl.ds(own_place(), 1), :]
    parity = spread(row, 0)
    turns = [(spread(row, 1 + 2 * m), spread(row, 2 + 2 * m)) for m in range(2)]
    blocks = len(woven)
    for b in range(blocks):
        factors = [(spread(row, 5 + 8 * b + 2 * m), spread(row, 6 + 8 * b + 2 * m)) for m in range(4)]
        for r in range(b * rows // blocks, (b + 1) * rows // blocks, SUB):
            if woven[b]:
                values = [(ref[pl.ds(2 * r, SUB, 2), :], ref[pl.ds(2 * r + 1, SUB, 2), :]) for ref in ins]
            else:
                values = [(ref[r : r + SUB, :], ref[rows + r : rows + r + SUB, :]) for ref in ins]
            (r0, i0), (r1, i1), (r2, i2), (r3, i3) = values
            r2, i2, r3, i3 = r2 * parity, i2 * parity, r3 * parity, i3 * parity
            results = [None] * 4
            for m, (pr, pi, qr, qi) in enumerate(
                ((r0 + r2, i0 + i2, r1 + r3, i1 + i3), (r0 - r2, i0 - i2, r1 - r3, i1 - i3))
            ):
                tc, ts = turns[m]
                tr, ti = qr * tc - qi * ts, qr * ts + qi * tc
                results[m], results[m + 2] = (pr + tr, pi + ti), (pr - tr, pi - ti)
            for out, (re, im), (c, s) in zip(outs, results, factors):
                out[r : r + SUB, :] = re * c - im * s
                out[rows + r : rows + r + SUB, :] = re * s + im * c


def mix(parts, woven, table):
    work = sum(part.size for part in parts)
    mixed = pl.pallas_call(
        functools.partial(mix_kernel, woven),
        in_specs=[VMEM_WHOLE] * 5,
        out_shape=[jax.ShapeDtypeStruct(parts[0].shape, jnp.float32)] * 4,
        cost_estimate=pl.CostEstimate(flops=8 * work, bytes_accessed=8 * work, transcendentals=0),
        compiler_params=pltpu.CompilerParams(vmem_limit_bytes=16 << 20),
    )(table, *[parts[m] for m in FAR_FIRST])
    return [mixed[FAR_FIRST.index(m)] for m in range(4)]


def quarter_kernel(start, in_ref, *refs):
    out_refs, sems = refs[:-1], refs[-1]
    quarter = in_ref.shape[1] // len(out_refs)
    group = lax.axis_index("grp")
    copies = []
    for m, out_ref in enumerate(out_refs):
        at = pl.multiple_of((group ^ m) * quarter + start, LANES)
        copies.append(pltpu.make_async_copy(in_ref.at[:, pl.ds(at, out_ref.shape[1])], out_ref, sems.at[m]))
        copies[-1].start()
    for copy in copies:
        copy.wait()


def quarters(series, start, size):
    parts = pl.pallas_call(
        functools.partial(quarter_kernel, start),
        in_specs=[pl.BlockSpec(memory_space=pltpu.HBM)],
        out_specs=[VMEM_WHOLE] * 4,
        out_shape=[jax.ShapeDtypeStruct((2, size), jnp.float32)] * 4,
        scratch_shapes=[pltpu.SemaphoreType.DMA((4,))],
        compiler_params=pltpu.CompilerParams(vmem_limit_bytes=8 << 20),
    )(pltpu.with_memory_space_constraint(series, pltpu.HBM))
    return [part.reshape(2, size // LANES, LANES).transpose(1, 0, 2).reshape(-1, LANES) for part in parts]


def swap(parts, shift):
    return [send(part, m << shift) if m else part for m, part in enumerate(parts)]


def send(part, flip):
    return lax.ppermute(part, AXES, [(d, d ^ flip) for d in range(lax.axis_size(AXES))])


def device_digits():
    d = np.arange(32)
    z, yx, core = d // 8, d // 2 % 4, d % 2
    return z, yx, core, yx + 4 * z + 16 * core


def root(product, modulus):
    c, s = roots(product, modulus)
    return c + 1j * s


def rows_of(columns):
    flat = [columns[0].real] + [part for column in columns[1:] for part in (column.real, column.imag)]
    table = np.zeros((32, LANES), np.float32)
    table[:, : len(flat)] = np.stack(flat, 1)
    return table


def mix_table(mine, digit, factors):
    columns = [root((mine ^ 2) * digit - mine * digit, 4)]
    columns += [root(((mine ^ 1) - mine) * (digit ^ m), 4) for m in range(2)]
    return rows_of(columns + [f * root(mine * (digit ^ m), 4) for block in factors for m, f in enumerate(block)])


def mix_tables(points, start, rows):
    z, yx, core, _ = device_digits()
    first = [[root((2 * yx + core) * (yx ^ m), 32) / math.sqrt(points) for m in range(4)]]
    second = [
        [root(core * (z ^ m), 8) * root((yx + 4 * (z ^ m)) * (z * 8 + start // 32 + b), 1024) for m in range(4)]
        for b in range(rows // 32)
    ]
    return mix_table(z, yx, first), mix_table(yx, z, second)


def slab_kernel(starts, bit_ref, near_ref, mid_ref, turn_ref, fh_ref, fl_ref, *refs):
    in_refs, (out_ref, whole, first, second) = refs[:-4], refs[-4:]
    place = own_place()
    group, pair, core = place // 8, place // 2 % 4, place % 2
    digit = pair + 4 * group + 16 * core
    row = bit_ref[pl.ds(place, 1), :]
    sign = spread(row, 0)
    span, block = 1024, 0
    for h, start in enumerate(starts):
        for m in range(4):
            mine, other = in_refs[h * 8 + FAR_FIRST.index(m)], in_refs[h * 8 + 4 + FAR_FIRST.index(m)]
            rows = mine.shape[0] // 2
            at = pl.multiple_of((group ^ m) * (span // 4) + start, 32)
            for b in range(0, rows, 32):
                c, s = spread(row, 1 + 2 * block), spread(row, 2 + 2 * block)
                block += 1
                for r in range(b, b + 32, SUB):
                    re = other[r : r + SUB, :] + mine[r : r + SUB, :] * sign
                    im = other[rows + r : rows + r + SUB, :] + mine[rows + r : rows + r + SUB, :] * sign
                    whole[pl.ds(at + r, SUB), :] = re * c - im * s
                    whole[pl.ds(span + at + r, SUB), :] = re * s + im * c
    outer = inner = 32
    for j in range(0, inner, SUB):
        values = []
        for e in range(outer):
            base = e * inner + j
            values.append((whole[base : base + SUB, :], whole[span + base : span + base + SUB, :]))
        at = pl.multiple_of(digit * 2 * inner + j, SUB)
        nc, ns = near_ref[pl.ds(at, SUB), :], near_ref[pl.ds(at + inner, SUB), :]
        for k, (re, im) in enumerate(dft_list(values)):
            base = k * inner + j
            mc, ms = mid_ref[base : base + SUB, :], mid_ref[span + base : span + base + SUB, :]
            c, s = mc * nc - ms * ns, mc * ns + ms * nc
            first[base : base + SUB, :] = re * c - im * s
            first[span + base : span + base + SUB, :] = re * s + im * c
    lane_stage(outer, inner, turn_ref, fh_ref, fl_ref, out_ref, first, second)


def slab_transform(arrived, lane_rows, points):
    z, _, core, _ = device_digits()
    nc, ns = roots(np.arange(32)[:, None] * np.arange(32 * LANES)[None, :], points)
    near = np.stack([nc, ns], 1).reshape(32 * 2 * 32, LANES).astype(np.float32)
    mid, turn, fh, fl, _ = local_tables(32, 32, lane_rows)
    starts = [sum(CHUNKS[:h]) for h in range(len(CHUNKS))]
    bits = [1 - 2 * core + 0j]
    for start, rows in zip(starts, CHUNKS):
        for m in range(4):
            bits += [root(core * ((z ^ m) * 8 + start // 32 + b), 64) for b in range(rows // 32)]
    return pl.pallas_call(
        functools.partial(slab_kernel, starts),
        in_specs=[VMEM_WHOLE] * (6 + len(arrived)),
        out_shape=jax.ShapeDtypeStruct((32, 64, LANES), jnp.float32),
        scratch_shapes=[
            pltpu.VMEM((2048, LANES), jnp.float32),
            pltpu.VMEM((2048, LANES), jnp.float32),
            pltpu.VMEM((1024, 2 * LANES), jnp.float32),
        ],
        compiler_params=pltpu.CompilerParams(vmem_limit_bytes=20 << 20),
    )(rows_of(bits), near, mid, turn, fh, fl, *arrived)


CHUNKS = (96, 160)


def after(arrays, result):
    return list(lax.optimization_barrier((*arrays, result)))[:-1]


def by_axes(series, points):
    slab = series.shape[1]
    starts = [sum(CHUNKS[:h]) for h in range(len(CHUNKS))]
    tables = [mix_tables(points, start, rows) for start, rows in zip(starts, CHUNKS)]
    one, two = [quarters(series, start * LANES, rows * LANES) for start, rows in zip(starts, CHUNKS)]
    one = swap(one, 3)
    two = swap(two, 3)
    one = mix(one, (True,), tables[0][0])
    one = swap(one, 1)
    one = after(one, two[2])
    one = mix(one, (False,) * (CHUNKS[0] // 32), tables[0][1])
    one = swap(one, 3)
    two = mix(two, (True,), tables[1][0])
    two = swap(two, 1)
    two = mix(two, (False,) * (CHUNKS[1] // 32), tables[1][1])
    two = swap(two, 3)
    arrived = []
    for parts in (one, two):
        mine = [parts[m] for m in FAR_FIRST]
        arrived += mine + [send(part, 1) for part in mine]
    dest, c, low = np.meshgrid(np.arange(32), np.arange(2), np.arange(4), indexing="ij")
    lane_rows = ((dest * 4 + low).reshape(-1), (c == 1).reshape(-1))
    spectrum = slab_transform(arrived, lane_rows, points)
    landed = lax.all_to_all(spectrum, AXES, split_axis=0, concat_axis=0, tiled=True).reshape(2048, LANES)
    ordered = order_rows(landed, np.argsort(device_digits()[3]).tolist())
    return ordered.reshape(slab // LANES, 2, LANES).transpose(1, 0, 2).reshape(2, slab)


def exchange(blocks, count):
    shape = blocks.shape
    blocks = blocks.reshape((count, shape[0] // count) + shape[1:])
    return lax.all_to_all(blocks, ORDER, split_axis=0, concat_axis=0, tiled=True).reshape(shape)


def local(series):
    count = lax.axis_size("grp") * lax.axis_size("dev")
    slab = series.shape[1]
    points = slab * count
    piece_rows = slab // count // LANES
    if (lax.axis_size("grp"), lax.axis_size("dev"), slab) == (4, 8, 1024 * LANES):
        return by_axes(series, points)
    at = np.arange(count).reshape(lax.axis_size("dev"), lax.axis_size("grp")).T.reshape(-1)
    owners = np.argsort(at)
    tiles = series.reshape(2, count, piece_rows, LANES).transpose(1, 2, 0, 3)
    received = exchange(tiles, count).reshape(2 * slab // LANES, LANES)
    turned = across(received, at.tolist(), points, 1.0 / math.sqrt(points))
    arrived = exchange(turned, count)
    if 2 * LANES == SUB * count:
        lows = LANES // count
        dest, c, low = np.meshgrid(owners, np.arange(2), np.arange(lows), indexing="ij")
        lane_rows = ((dest * lows + low).reshape(-1), (c == 1).reshape(-1))
        spectrum, _ = local_transform(arrived, count, piece_rows, lane_rows)
        landed = exchange(spectrum.reshape(turned.shape), count)
        ordered = order_rows(landed, list(range(count)))
        return ordered.reshape(slab // LANES, 2, LANES).transpose(1, 0, 2).reshape(2, slab)
    freq, c = np.meshgrid(np.arange(LANES), np.arange(2), indexing="ij")
    spectrum, kept = local_transform(arrived, count, piece_rows, (freq.reshape(-1), (c == 1).reshape(-1)))
    spectrum = spectrum.reshape(2 * LANES // SUB, -1, SUB, LANES).transpose(0, 2, 1, 3).reshape(2 * LANES, -1)
    natural = jnp.take(spectrum, np.argsort(kept), axis=1).reshape(LANES, 2, -1)
    blocks = natural.transpose(0, 2, 1).reshape(count, -1, 2)[owners]
    landed = exchange(blocks, count)
    return landed.transpose(2, 1, 0).reshape(2, slab)


def solution(mesh):
    return jax.shard_map(
        local,
        mesh=mesh,
        in_specs=(P(None, AXES),),
        out_specs=P(None, AXES),
        check_vma=False,
    )
```

```python
import functools
import math

import jax
import jax.numpy as jnp
import numpy as np
from jax import lax
from jax.experimental import pallas as pl
from jax.experimental.pallas import tpu as pltpu
from jax.sharding import PartitionSpec as P

LANES = 128
SUB = 8
AXES = ("grp", "dev")
ORDER = ("dev", "grp")


def roots(product, modulus):
    angle = np.asarray(product, np.int64) % modulus * (-2.0 * math.pi / modulus)
    return np.cos(angle), np.sin(angle)


def times_root(value, k, n):
    re, im = value
    k %= n
    if k == 0:
        return value
    if 4 * k == n:
        return im, -re
    if 2 * k == n:
        return -re, -im
    if 4 * k == 3 * n:
        return -im, re
    if 8 * k == n:
        half = np.float32(math.sqrt(0.5))
        return (re + im) * half, (im - re) * half
    if 8 * k == 3 * n:
        half = np.float32(math.sqrt(0.5))
        return (im - re) * half, (re + im) * -half
    angle = -2.0 * math.pi * k / n
    c, s = np.float32(math.cos(angle)), np.float32(math.sin(angle))
    return re * c - im * s, re * s + im * c


def dft_list(values):
    n = len(values)
    if n == 1:
        return values
    even, odd = dft_list(values[0::2]), dft_list(values[1::2])
    low, high = [], []
    for k in range(n // 2):
        (er, ei), (tr, ti) = even[k], times_root(odd[k], k, n)
        low.append((er + tr, ei + ti))
        high.append((er - tr, ei - ti))
    return low + high


def across_kernel(sources, place_ref, turn_ref, step_ref, in_ref, out_ref):
    count = len(sources)
    rows = in_ref.shape[0] // count // 2
    for j in range(0, rows, SUB):
        take = min(SUB, rows - j)
        values = []
        for at in sources:
            base = (at * rows + j) * 2
            values.append((in_ref[pl.ds(base, take, 2), :], in_ref[pl.ds(base + 1, take, 2), :]))
        for k, (re, im) in enumerate(dft_list(values)):
            base = k * 2 * rows + j
            tc, ts = turn_ref[base : base + take, :], turn_ref[base + rows : base + rows + take, :]
            dc, ds = step_ref[0, 2 * k], step_ref[0, 2 * k + 1]
            c, s = tc * dc - ts * ds, tc * ds + ts * dc
            out_ref[base : base + take, :] = re * c - im * s
            out_ref[base + rows : base + rows + take, :] = re * s + im * c


def across(received, sources, points, scale):
    count = len(sources)
    slab = points // count
    piece = slab // count
    digits = np.arange(count)
    tc, ts = roots(digits[:, None] * np.arange(piece)[None, :], points)
    turn = np.stack([tc, ts], 1).reshape(count * 2 * piece // LANES, LANES) * scale
    dc, ds = roots(digits[:, None] * digits[None, :], count * count)
    step = np.stack([dc, ds], 2).reshape(count, 1, 2 * count)
    place = lax.axis_index(ORDER).astype(jnp.int32).reshape(1)
    whole = pl.BlockSpec(received.shape, lambda i, place: (0, 0))
    return pl.pallas_call(
        functools.partial(across_kernel, sources),
        grid_spec=pltpu.PrefetchScalarGridSpec(
            num_scalar_prefetch=1,
            grid=(1,),
            in_specs=[
                whole,
                pl.BlockSpec((None, 1, 2 * count), lambda i, place: (place[0], 0, 0), memory_space=pltpu.SMEM),
                whole,
            ],
            out_specs=whole,
        ),
        out_shape=jax.ShapeDtypeStruct(received.shape, jnp.float32),
        compiler_params=pltpu.CompilerParams(vmem_limit_bytes=32 << 20),
    )(place, turn.astype(np.float32), step.astype(np.float32), received)


def split_bf16(values):
    high = values.astype(jnp.bfloat16)
    return high, (values - high.astype(jnp.float32)).astype(jnp.bfloat16)


def first_pitch(outer, inner):
    return outer // SUB * inner + SUB


def lane_stage(outer, inner, turn_ref, fh_ref, fl_ref, out_ref, first, second):
    span = outer * inner
    fold, pitch = outer // SUB, first_pitch(outer, inner)
    together = max(1, LANES // (inner * SUB))
    dot = functools.partial(
        lax.dot_general, dimension_numbers=(((1,), (1,)), ((), ())), preferred_element_type=jnp.float32
    )
    for begin in range(0, fold, together):
        for v in range(begin, begin + together):
            values = []
            for j in range(inner):
                at = v * inner + j
                values.append((first[pl.ds(at, SUB, pitch), :], first[pl.ds(SUB * pitch + at, SUB, pitch), :]))
            for k, (re, im) in enumerate(dft_list(values)):
                base = (v * inner + k) * SUB
                c, s = turn_ref[base : base + SUB, :], turn_ref[span + base : span + base + SUB, :]
                second[base : base + SUB, :LANES] = re * c - im * s
                second[base : base + SUB, LANES:] = re * s + im * c
        columns = together * inner * SUB
        done = begin * inner * SUB
        xh, xl = split_bf16(second[done : done + columns, :])
        result = dot(fh_ref[...], xh) + (dot(fh_ref[...], xl) + dot(fl_ref[...], xh))
        for t in range(columns // LANES):
            tile = result[:, t * LANES : (t + 1) * LANES]
            at = (done // LANES + t) * SUB
            out_ref[:, at : at + SUB, :] = tile.reshape(tile.shape[0] // SUB, SUB, LANES)


def local_kernel(piece_rows, mid_ref, turn_ref, fh_ref, fl_ref, in_ref, out_ref, first, second):
    inner = piece_rows
    outer = in_ref.shape[0] // 2 // inner
    span = outer * inner
    fold, pitch = outer // SUB, first_pitch(outer, inner)
    for j in range(0, inner, SUB):
        take = min(SUB, inner - j)
        values = []
        for e in range(outer):
            base = e * 2 * inner + j
            values.append((in_ref[base : base + take, :], in_ref[base + inner : base + inner + take, :]))
        for k, (re, im) in enumerate(dft_list(values)):
            base = k * inner + j
            c, s = mid_ref[base : base + take, :], mid_ref[span + base : span + base + take, :]
            at = k // fold * pitch + k % fold * inner + j
            first[at : at + take, :] = re * c - im * s
            first[SUB * pitch + at : SUB * pitch + at + take, :] = re * s + im * c
    lane_stage(outer, inner, turn_ref, fh_ref, fl_ref, out_ref, first, second)


def local_tables(outer, inner, lane_rows):
    span = outer * inner
    slab = span * LANES
    mc, ms = roots(np.arange(outer)[:, None] * np.arange(inner)[None, :], span)
    mid = np.broadcast_to(np.stack([mc, ms]).reshape(2 * span, 1), (2 * span, LANES))
    fold = outer // SUB
    v, k, i = np.meshgrid(np.arange(fold), np.arange(inner), np.arange(SUB), indexing="ij")
    kept = ((v + fold * i) + outer * k).reshape(span)
    tc, ts = roots(kept[:, None] * np.arange(LANES)[None, :], slab)
    turn = np.concatenate([tc, ts])
    freq, imag = lane_rows
    fc, fs = roots(freq[:, None] * np.arange(LANES)[None, :], LANES)
    lane = np.where(imag[:, None], np.concatenate([fs, fc], 1), np.concatenate([fc, -fs], 1)).astype(np.float32)
    fh = lane.astype(jnp.bfloat16)
    fl = (lane - fh.astype(np.float32)).astype(jnp.bfloat16)
    return mid.astype(np.float32), turn.astype(np.float32), fh, fl, kept


def local_transform(arrived, outer, inner, lane_rows):
    span = outer * inner
    mid, turn, fh, fl, kept = local_tables(outer, inner, lane_rows)
    return pl.pallas_call(
        functools.partial(local_kernel, inner),
        out_shape=jax.ShapeDtypeStruct((2 * LANES // SUB, SUB * span // LANES, LANES), jnp.float32),
        scratch_shapes=[
            pltpu.VMEM((2 * SUB * first_pitch(outer, inner), LANES), jnp.float32),
            pltpu.VMEM((span, 2 * LANES), jnp.float32),
        ],
        compiler_params=pltpu.CompilerParams(vmem_limit_bytes=20 << 20),
    )(mid, turn, fh, fl, arrived), kept


def order_kernel(sources, in_ref, out_ref, whole, ordered, sems):
    count = len(sources)
    fold = LANES // count
    each = in_ref.shape[0] // count
    tiles = each // SUB // fold
    lows = SUB // 2
    rows = tiles * LANES * 2
    pitch = each + SUB
    for k, at in enumerate(sources):
        whole[k * pitch : k * pitch + each, :] = in_ref[at * each : (at + 1) * each, :]
    copies = []
    for low in range(lows):
        for t in range(tiles):
            base = low * rows + t * LANES * 2
            for c in range(2):
                parts = [
                    whole[pl.ds((v * tiles + t) * SUB + c * lows + low, count, pitch), :] for v in range(fold)
                ]
                ordered[pl.ds(base + c, LANES, 2), :] = jnp.concatenate(parts, 0).T
            piece = pl.ds(base, LANES * 2)
            copies.append(pltpu.make_async_copy(ordered.at[piece, :], out_ref.at[piece, :], sems.at[low, t]))
            copies[-1].start()
    for copy in copies:
        copy.wait()


def order_rows(landed, sources):
    return pl.pallas_call(
        functools.partial(order_kernel, sources),
        in_specs=[pl.BlockSpec(memory_space=pltpu.VMEM)],
        out_specs=pl.BlockSpec(memory_space=pltpu.HBM),
        out_shape=jax.ShapeDtypeStruct(landed.shape, jnp.float32),
        scratch_shapes=[
            pltpu.VMEM((landed.shape[0] + SUB * len(sources), LANES), jnp.float32),
            pltpu.VMEM(landed.shape, jnp.float32),
            pltpu.SemaphoreType.DMA((SUB // 2, landed.shape[0] // SUB // LANES)),
        ],
        compiler_params=pltpu.CompilerParams(vmem_limit_bytes=16 << 20),
    )(landed)


VMEM_WHOLE = pl.BlockSpec(memory_space=pltpu.VMEM)
FAR_FIRST = (0, 2, 3, 1)


def own_place():
    return lax.axis_index("grp") * 8 + lax.axis_index("dev")


def spread(row, at):
    return jnp.broadcast_to(row[:, at : at + 1], (SUB, LANES))


def mix_kernel(woven, coef_ref, *refs):
    ins, outs = [None] * 4, [None] * 4
    for n, m in enumerate(FAR_FIRST):
        ins[m], outs[m] = refs[n], refs[4 + n]
    rows = refs[0].shape[0] // 2
    row = coef_ref[pl.ds(own_place(), 1), :]
    parity = spread(row, 0)
    turns = [(spread(row, 1 + 2 * m), spread(row, 2 + 2 * m)) for m in range(2)]
    blocks = len(woven)
    for b in range(blocks):
        factors = [(spread(row, 5 + 8 * b + 2 * m), spread(row, 6 + 8 * b + 2 * m)) for m in range(4)]
        for r in range(b * rows // blocks, (b + 1) * rows // blocks, SUB):
            if woven[b]:
                values = [(ref[pl.ds(2 * r, SUB, 2), :], ref[pl.ds(2 * r + 1, SUB, 2), :]) for ref in ins]
            else:
                values = [(ref[r : r + SUB, :], ref[rows + r : rows + r + SUB, :]) for ref in ins]
            (r0, i0), (r1, i1), (r2, i2), (r3, i3) = values
            r2, i2, r3, i3 = r2 * parity, i2 * parity, r3 * parity, i3 * parity
            results = [None] * 4
            for m, (pr, pi, qr, qi) in enumerate(
                ((r0 + r2, i0 + i2, r1 + r3, i1 + i3), (r0 - r2, i0 - i2, r1 - r3, i1 - i3))
            ):
                tc, ts = turns[m]
                tr, ti = qr * tc - qi * ts, qr * ts + qi * tc
                results[m], results[m + 2] = (pr + tr, pi + ti), (pr - tr, pi - ti)
            for out, (re, im), (c, s) in zip(outs, results, factors):
                out[r : r + SUB, :] = re * c - im * s
                out[rows + r : rows + r + SUB, :] = re * s + im * c


def mix(parts, woven, table):
    work = sum(part.size for part in parts)
    mixed = pl.pallas_call(
        functools.partial(mix_kernel, woven),
        in_specs=[VMEM_WHOLE] * 5,
        out_shape=[jax.ShapeDtypeStruct(parts[0].shape, jnp.float32)] * 4,
        cost_estimate=pl.CostEstimate(flops=8 * work, bytes_accessed=8 * work, transcendentals=0),
        compiler_params=pltpu.CompilerParams(vmem_limit_bytes=16 << 20),
    )(table, *[parts[m] for m in FAR_FIRST])
    return [mixed[FAR_FIRST.index(m)] for m in range(4)]


def quarter_kernel(start, in_ref, *refs):
    out_refs, sems = refs[:-1], refs[-1]
    quarter = in_ref.shape[1] // len(out_refs)
    group = lax.axis_index("grp")
    copies = []
    for m, out_ref in enumerate(out_refs):
        at = pl.multiple_of((group ^ m) * quarter + start, LANES)
        copies.append(pltpu.make_async_copy(in_ref.at[:, pl.ds(at, out_ref.shape[1])], out_ref, sems.at[m]))
        copies[-1].start()
    for copy in copies:
        copy.wait()


def quarters(series, start, size):
    parts = pl.pallas_call(
        functools.partial(quarter_kernel, start),
        in_specs=[pl.BlockSpec(memory_space=pltpu.HBM)],
        out_specs=[VMEM_WHOLE] * 4,
        out_shape=[jax.ShapeDtypeStruct((2, size), jnp.float32)] * 4,
        scratch_shapes=[pltpu.SemaphoreType.DMA((4,))],
        compiler_params=pltpu.CompilerParams(vmem_limit_bytes=8 << 20),
    )(pltpu.with_memory_space_constraint(series, pltpu.HBM))
    return [part.reshape(2, size // LANES, LANES).transpose(1, 0, 2).reshape(-1, LANES) for part in parts]


def swap(parts, shift):
    return [send(part, m << shift) if m else part for m, part in enumerate(parts)]


def send(part, flip):
    return lax.ppermute(part, AXES, [(d, d ^ flip) for d in range(lax.axis_size(AXES))])


def device_digits():
    d = np.arange(32)
    z, yx, core = d // 8, d // 2 % 4, d % 2
    return z, yx, core, yx + 4 * z + 16 * core


def root(product, modulus):
    c, s = roots(product, modulus)
    return c + 1j * s


def rows_of(columns):
    flat = [columns[0].real] + [part for column in columns[1:] for part in (column.real, column.imag)]
    table = np.zeros((32, LANES), np.float32)
    table[:, : len(flat)] = np.stack(flat, 1)
    return table


def mix_table(mine, digit, factors):
    columns = [root((mine ^ 2) * digit - mine * digit, 4)]
    columns += [root(((mine ^ 1) - mine) * (digit ^ m), 4) for m in range(2)]
    return rows_of(columns + [f * root(mine * (digit ^ m), 4) for block in factors for m, f in enumerate(block)])


def mix_tables(points, start, rows):
    z, yx, core, _ = device_digits()
    first = [[root((2 * yx + core) * (yx ^ m), 32) / math.sqrt(points) for m in range(4)]]
    second = [
        [root(core * (z ^ m), 8) * root((yx + 4 * (z ^ m)) * (z * 8 + start // 32 + b), 1024) for m in range(4)]
        for b in range(rows // 32)
    ]
    return mix_table(z, yx, first), mix_table(yx, z, second)


def slab_kernel(starts, bit_ref, near_ref, mid_ref, turn_ref, fh_ref, fl_ref, *refs):
    in_refs, (out_ref, whole, first, second) = refs[:-4], refs[-4:]
    place = own_place()
    group, pair, core = place // 8, place // 2 % 4, place % 2
    digit = pair + 4 * group + 16 * core
    row = bit_ref[pl.ds(place, 1), :]
    sign = spread(row, 0)
    span, block = 1024, 0
    for h, start in enumerate(starts):
        for m in range(4):
            mine, other = in_refs[h * 8 + FAR_FIRST.index(m)], in_refs[h * 8 + 4 + FAR_FIRST.index(m)]
            rows = mine.shape[0] // 2
            at = pl.multiple_of((group ^ m) * (span // 4) + start, 32)
            for b in range(0, rows, 32):
                c, s = spread(row, 1 + 2 * block), spread(row, 2 + 2 * block)
                block += 1
                for r in range(b, b + 32, SUB):
                    re = other[r : r + SUB, :] + mine[r : r + SUB, :] * sign
                    im = other[rows + r : rows + r + SUB, :] + mine[rows + r : rows + r + SUB, :] * sign
                    whole[pl.ds(at + r, SUB), :] = re * c - im * s
                    whole[pl.ds(span + at + r, SUB), :] = re * s + im * c
    outer = inner = 32
    fold, pitch = outer // SUB, first_pitch(outer, inner)
    for j in range(0, inner, SUB):
        values = []
        for e in range(outer):
            base = e * inner + j
            values.append((whole[base : base + SUB, :], whole[span + base : span + base + SUB, :]))
        at = pl.multiple_of(digit * 2 * inner + j, SUB)
        nc, ns = near_ref[pl.ds(at, SUB), :], near_ref[pl.ds(at + inner, SUB), :]
        for k, (re, im) in enumerate(dft_list(values)):
            base = k * inner + j
            mc, ms = mid_ref[base : base + SUB, :], mid_ref[span + base : span + base + SUB, :]
            c, s = mc * nc - ms * ns, mc * ns + ms * nc
            at = k // fold * pitch + k % fold * inner + j
            first[at : at + SUB, :] = re * c - im * s
            first[SUB * pitch + at : SUB * pitch + at + SUB, :] = re * s + im * c
    lane_stage(outer, inner, turn_ref, fh_ref, fl_ref, out_ref, first, second)


def slab_transform(arrived, lane_rows, points):
    z, _, core, _ = device_digits()
    nc, ns = roots(np.arange(32)[:, None] * np.arange(32 * LANES)[None, :], points)
    near = np.stack([nc, ns], 1).reshape(32 * 2 * 32, LANES).astype(np.float32)
    mid, turn, fh, fl, _ = local_tables(32, 32, lane_rows)
    starts = [sum(CHUNKS[:h]) for h in range(len(CHUNKS))]
    bits = [1 - 2 * core + 0j]
    for start, rows in zip(starts, CHUNKS):
        for m in range(4):
            bits += [root(core * ((z ^ m) * 8 + start // 32 + b), 64) for b in range(rows // 32)]
    return pl.pallas_call(
        functools.partial(slab_kernel, starts),
        in_specs=[VMEM_WHOLE] * (6 + len(arrived)),
        out_shape=jax.ShapeDtypeStruct((32, 64, LANES), jnp.float32),
        scratch_shapes=[
            pltpu.VMEM((2048, LANES), jnp.float32),
            pltpu.VMEM((2 * SUB * first_pitch(32, 32), LANES), jnp.float32),
            pltpu.VMEM((1024, 2 * LANES), jnp.float32),
        ],
        compiler_params=pltpu.CompilerParams(vmem_limit_bytes=20 << 20),
    )(rows_of(bits), near, mid, turn, fh, fl, *arrived)


CHUNKS = (96, 160)


def after(arrays, result):
    return list(lax.optimization_barrier((*arrays, result)))[:-1]


def by_axes(series, points):
    slab = series.shape[1]
    starts = [sum(CHUNKS[:h]) for h in range(len(CHUNKS))]
    tables = [mix_tables(points, start, rows) for start, rows in zip(starts, CHUNKS)]
    one, two = [quarters(series, start * LANES, rows * LANES) for start, rows in zip(starts, CHUNKS)]
    one = swap(one, 3)
    two = swap(two, 3)
    one = mix(one, (True,), tables[0][0])
    one = swap(one, 1)
    one = after(one, two[2])
    one = mix(one, (False,) * (CHUNKS[0] // 32), tables[0][1])
    one = swap(one, 3)
    two = mix(two, (True,), tables[1][0])
    two = swap(two, 1)
    two = mix(two, (False,) * (CHUNKS[1] // 32), tables[1][1])
    two = swap(two, 3)
    arrived = []
    for parts in (one, two):
        mine = [parts[m] for m in FAR_FIRST]
        arrived += mine + [send(part, 1) for part in mine]
    at = np.arange(32).reshape(8, 4).T.reshape(-1)
    dest, c, low = np.meshgrid(np.argsort(at), np.arange(2), np.arange(4), indexing="ij")
    lane_rows = ((dest * 4 + low).reshape(-1), (c == 1).reshape(-1))
    spectrum = slab_transform(arrived, lane_rows, points)
    landed = lax.all_to_all(spectrum, ORDER, split_axis=0, concat_axis=0, tiled=True).reshape(2048, LANES)
    ordered = order_rows(landed, at[np.argsort(device_digits()[3])].tolist())
    return ordered.reshape(slab // LANES, 2, LANES).transpose(1, 0, 2).reshape(2, slab)


def exchange(blocks, count):
    shape = blocks.shape
    blocks = blocks.reshape((count, shape[0] // count) + shape[1:])
    return lax.all_to_all(blocks, ORDER, split_axis=0, concat_axis=0, tiled=True).reshape(shape)


def local(series):
    count = lax.axis_size("grp") * lax.axis_size("dev")
    slab = series.shape[1]
    points = slab * count
    piece_rows = slab // count // LANES
    if (lax.axis_size("grp"), lax.axis_size("dev"), slab) == (4, 8, 1024 * LANES):
        return by_axes(series, points)
    at = np.arange(count).reshape(lax.axis_size("dev"), lax.axis_size("grp")).T.reshape(-1)
    owners = np.argsort(at)
    tiles = series.reshape(2, count, piece_rows, LANES).transpose(1, 2, 0, 3)
    received = exchange(tiles, count).reshape(2 * slab // LANES, LANES)
    turned = across(received, at.tolist(), points, 1.0 / math.sqrt(points))
    arrived = exchange(turned, count)
    if 2 * LANES == SUB * count:
        lows = LANES // count
        dest, c, low = np.meshgrid(owners, np.arange(2), np.arange(lows), indexing="ij")
        lane_rows = ((dest * lows + low).reshape(-1), (c == 1).reshape(-1))
        spectrum, _ = local_transform(arrived, count, piece_rows, lane_rows)
        landed = exchange(spectrum.reshape(turned.shape), count)
        ordered = order_rows(landed, list(range(count)))
        return ordered.reshape(slab // LANES, 2, LANES).transpose(1, 0, 2).reshape(2, slab)
    freq, c = np.meshgrid(np.arange(LANES), np.arange(2), indexing="ij")
    spectrum, kept = local_transform(arrived, count, piece_rows, (freq.reshape(-1), (c == 1).reshape(-1)))
    spectrum = spectrum.reshape(2 * LANES // SUB, -1, SUB, LANES).transpose(0, 2, 1, 3).reshape(2 * LANES, -1)
    natural = jnp.take(spectrum, np.argsort(kept), axis=1).reshape(LANES, 2, -1)
    blocks = natural.transpose(0, 2, 1).reshape(count, -1, 2)[owners]
    landed = exchange(blocks, count)
    return landed.transpose(2, 1, 0).reshape(2, slab)


def solution(mesh):
    return jax.shard_map(
        local,
        mesh=mesh,
        in_specs=(P(None, AXES),),
        out_specs=P(None, AXES),
        check_vma=False,
    )
```

```python
import functools
import math

import jax
import jax.numpy as jnp
import numpy as np
from jax import lax
from jax.experimental import pallas as pl
from jax.experimental.pallas import tpu as pltpu
from jax.sharding import PartitionSpec as P

LANES = 128
SUB = 8
AXES = ("grp", "dev")
ORDER = ("dev", "grp")


def roots(product, modulus):
    angle = np.asarray(product, np.int64) % modulus * (-2.0 * math.pi / modulus)
    return np.cos(angle), np.sin(angle)


def times_root(value, k, n):
    re, im = value
    k %= n
    if k == 0:
        return value
    if 4 * k == n:
        return im, -re
    if 2 * k == n:
        return -re, -im
    if 4 * k == 3 * n:
        return -im, re
    if 8 * k == n:
        half = np.float32(math.sqrt(0.5))
        return (re + im) * half, (im - re) * half
    if 8 * k == 3 * n:
        half = np.float32(math.sqrt(0.5))
        return (im - re) * half, (re + im) * -half
    angle = -2.0 * math.pi * k / n
    c, s = np.float32(math.cos(angle)), np.float32(math.sin(angle))
    return re * c - im * s, re * s + im * c


def dft_list(values):
    n = len(values)
    if n == 1:
        return values
    even, odd = dft_list(values[0::2]), dft_list(values[1::2])
    low, high = [], []
    for k in range(n // 2):
        (er, ei), (tr, ti) = even[k], times_root(odd[k], k, n)
        low.append((er + tr, ei + ti))
        high.append((er - tr, ei - ti))
    return low + high


def across_kernel(sources, place_ref, turn_ref, step_ref, in_ref, out_ref):
    count = len(sources)
    rows = in_ref.shape[0] // count // 2
    for j in range(0, rows, SUB):
        take = min(SUB, rows - j)
        values = []
        for at in sources:
            base = (at * rows + j) * 2
            values.append((in_ref[pl.ds(base, take, 2), :], in_ref[pl.ds(base + 1, take, 2), :]))
        for k, (re, im) in enumerate(dft_list(values)):
            base = k * 2 * rows + j
            tc, ts = turn_ref[base : base + take, :], turn_ref[base + rows : base + rows + take, :]
            dc, ds = step_ref[0, 2 * k], step_ref[0, 2 * k + 1]
            c, s = tc * dc - ts * ds, tc * ds + ts * dc
            out_ref[base : base + take, :] = re * c - im * s
            out_ref[base + rows : base + rows + take, :] = re * s + im * c


def across(received, sources, points, scale):
    count = len(sources)
    slab = points // count
    piece = slab // count
    digits = np.arange(count)
    tc, ts = roots(digits[:, None] * np.arange(piece)[None, :], points)
    turn = np.stack([tc, ts], 1).reshape(count * 2 * piece // LANES, LANES) * scale
    dc, ds = roots(digits[:, None] * digits[None, :], count * count)
    step = np.stack([dc, ds], 2).reshape(count, 1, 2 * count)
    place = lax.axis_index(ORDER).astype(jnp.int32).reshape(1)
    whole = pl.BlockSpec(received.shape, lambda i, place: (0, 0))
    return pl.pallas_call(
        functools.partial(across_kernel, sources),
        grid_spec=pltpu.PrefetchScalarGridSpec(
            num_scalar_prefetch=1,
            grid=(1,),
            in_specs=[
                whole,
                pl.BlockSpec((None, 1, 2 * count), lambda i, place: (place[0], 0, 0), memory_space=pltpu.SMEM),
                whole,
            ],
            out_specs=whole,
        ),
        out_shape=jax.ShapeDtypeStruct(received.shape, jnp.float32),
        compiler_params=pltpu.CompilerParams(vmem_limit_bytes=32 << 20),
    )(place, turn.astype(np.float32), step.astype(np.float32), received)


def split_bf16(values):
    high = values.astype(jnp.bfloat16)
    return high, (values - high.astype(jnp.float32)).astype(jnp.bfloat16)


def first_pitch(outer, inner):
    return outer // SUB * inner + SUB


def lane_stage(outer, inner, turn_ref, fh_ref, fl_ref, out_ref, first, second):
    span = outer * inner
    fold, pitch = outer // SUB, first_pitch(outer, inner)
    together = max(1, LANES // (inner * SUB))
    dot = functools.partial(
        lax.dot_general, dimension_numbers=(((1,), (1,)), ((), ())), preferred_element_type=jnp.float32
    )
    for begin in range(0, fold, together):
        for v in range(begin, begin + together):
            values = []
            for j in range(inner):
                at = v * inner + j
                values.append((first[pl.ds(at, SUB, pitch), :], first[pl.ds(SUB * pitch + at, SUB, pitch), :]))
            for k, (re, im) in enumerate(dft_list(values)):
                base = (v * inner + k) * SUB
                c, s = turn_ref[base : base + SUB, :], turn_ref[span + base : span + base + SUB, :]
                second[base : base + SUB, :LANES] = re * c - im * s
                second[base : base + SUB, LANES:] = re * s + im * c
        columns = together * inner * SUB
        done = begin * inner * SUB
        xh, xl = split_bf16(second[done : done + columns, :])
        result = dot(fh_ref[...], xh) + (dot(fh_ref[...], xl) + dot(fl_ref[...], xh))
        for t in range(columns // LANES):
            tile = result[:, t * LANES : (t + 1) * LANES]
            at = (done // LANES + t) * SUB
            out_ref[:, at : at + SUB, :] = tile.reshape(tile.shape[0] // SUB, SUB, LANES)


def local_kernel(piece_rows, mid_ref, turn_ref, fh_ref, fl_ref, in_ref, out_ref, first, second):
    inner = piece_rows
    outer = in_ref.shape[0] // 2 // inner
    span = outer * inner
    fold, pitch = outer // SUB, first_pitch(outer, inner)
    for j in range(0, inner, SUB):
        take = min(SUB, inner - j)
        values = []
        for e in range(outer):
            base = e * 2 * inner + j
            values.append((in_ref[base : base + take, :], in_ref[base + inner : base + inner + take, :]))
        for k, (re, im) in enumerate(dft_list(values)):
            base = k * inner + j
            c, s = mid_ref[base : base + take, :], mid_ref[span + base : span + base + take, :]
            at = k // fold * pitch + k % fold * inner + j
            first[at : at + take, :] = re * c - im * s
            first[SUB * pitch + at : SUB * pitch + at + take, :] = re * s + im * c
    lane_stage(outer, inner, turn_ref, fh_ref, fl_ref, out_ref, first, second)


def local_tables(outer, inner, lane_rows):
    span = outer * inner
    slab = span * LANES
    mc, ms = roots(np.arange(outer)[:, None] * np.arange(inner)[None, :], span)
    mid = np.broadcast_to(np.stack([mc, ms]).reshape(2 * span, 1), (2 * span, LANES))
    fold = outer // SUB
    v, k, i = np.meshgrid(np.arange(fold), np.arange(inner), np.arange(SUB), indexing="ij")
    kept = ((v + fold * i) + outer * k).reshape(span)
    tc, ts = roots(kept[:, None] * np.arange(LANES)[None, :], slab)
    turn = np.concatenate([tc, ts])
    freq, imag = lane_rows
    fc, fs = roots(freq[:, None] * np.arange(LANES)[None, :], LANES)
    lane = np.where(imag[:, None], np.concatenate([fs, fc], 1), np.concatenate([fc, -fs], 1)).astype(np.float32)
    fh = lane.astype(jnp.bfloat16)
    fl = (lane - fh.astype(np.float32)).astype(jnp.bfloat16)
    return mid.astype(np.float32), turn.astype(np.float32), fh, fl, kept


def local_transform(arrived, outer, inner, lane_rows):
    span = outer * inner
    mid, turn, fh, fl, kept = local_tables(outer, inner, lane_rows)
    return pl.pallas_call(
        functools.partial(local_kernel, inner),
        out_shape=jax.ShapeDtypeStruct((2 * LANES // SUB, SUB * span // LANES, LANES), jnp.float32),
        scratch_shapes=[
            pltpu.VMEM((2 * SUB * first_pitch(outer, inner), LANES), jnp.float32),
            pltpu.VMEM((span, 2 * LANES), jnp.float32),
        ],
        compiler_params=pltpu.CompilerParams(vmem_limit_bytes=20 << 20),
    )(mid, turn, fh, fl, arrived), kept


def order_kernel(sources, in_ref, out_ref, whole, ordered, sems):
    count = len(sources)
    fold = LANES // count
    each = in_ref.shape[0] // count
    tiles = each // SUB // fold
    lows = SUB // 2
    rows = tiles * LANES * 2
    pitch = each + SUB
    for k, at in enumerate(sources):
        whole[k * pitch : k * pitch + each, :] = in_ref[at * each : (at + 1) * each, :]
    copies = []
    for low in range(lows):
        for t in range(tiles):
            base = low * rows + t * LANES * 2
            for c in range(2):
                parts = [
                    whole[pl.ds((v * tiles + t) * SUB + c * lows + low, count, pitch), :] for v in range(fold)
                ]
                ordered[pl.ds(base + c, LANES, 2), :] = jnp.concatenate(parts, 0).T
            piece = pl.ds(base, LANES * 2)
            copies.append(pltpu.make_async_copy(ordered.at[piece, :], out_ref.at[piece, :], sems.at[low, t]))
            copies[-1].start()
    for copy in copies:
        copy.wait()


def order_rows(landed, sources):
    return pl.pallas_call(
        functools.partial(order_kernel, sources),
        in_specs=[pl.BlockSpec(memory_space=pltpu.VMEM)],
        out_specs=pl.BlockSpec(memory_space=pltpu.HBM),
        out_shape=jax.ShapeDtypeStruct(landed.shape, jnp.float32),
        scratch_shapes=[
            pltpu.VMEM((landed.shape[0] + SUB * len(sources), LANES), jnp.float32),
            pltpu.VMEM(landed.shape, jnp.float32),
            pltpu.SemaphoreType.DMA((SUB // 2, landed.shape[0] // SUB // LANES)),
        ],
        compiler_params=pltpu.CompilerParams(vmem_limit_bytes=16 << 20),
    )(landed)


VMEM_WHOLE = pl.BlockSpec(memory_space=pltpu.VMEM)
FAR_FIRST = (0, 2, 3, 1)


def own_place():
    return lax.axis_index("grp") * 8 + lax.axis_index("dev")


def spread(row, at):
    return jnp.broadcast_to(row[:, at : at + 1], (SUB, LANES))


def mix_kernel(woven, coef_ref, *refs):
    ins, outs = [None] * 4, [None] * 4
    for n, m in enumerate(FAR_FIRST):
        ins[m], outs[m] = refs[n], refs[4 + n]
    rows = refs[0].shape[0] // 2
    row = coef_ref[pl.ds(own_place(), 1), :]
    parity = spread(row, 0)
    turns = [(spread(row, 1 + 2 * m), spread(row, 2 + 2 * m)) for m in range(2)]
    blocks = len(woven)
    for b in range(blocks):
        factors = [(spread(row, 5 + 8 * b + 2 * m), spread(row, 6 + 8 * b + 2 * m)) for m in range(4)]
        for r in range(b * rows // blocks, (b + 1) * rows // blocks, SUB):
            if woven[b]:
                values = [(ref[pl.ds(2 * r, SUB, 2), :], ref[pl.ds(2 * r + 1, SUB, 2), :]) for ref in ins]
            else:
                values = [(ref[r : r + SUB, :], ref[rows + r : rows + r + SUB, :]) for ref in ins]
            (r0, i0), (r1, i1), (r2, i2), (r3, i3) = values
            r2, i2, r3, i3 = r2 * parity, i2 * parity, r3 * parity, i3 * parity
            results = [None] * 4
            for m, (pr, pi, qr, qi) in enumerate(
                ((r0 + r2, i0 + i2, r1 + r3, i1 + i3), (r0 - r2, i0 - i2, r1 - r3, i1 - i3))
            ):
                tc, ts = turns[m]
                tr, ti = qr * tc - qi * ts, qr * ts + qi * tc
                results[m], results[m + 2] = (pr + tr, pi + ti), (pr - tr, pi - ti)
            for out, (re, im), (c, s) in zip(outs, results, factors):
                out[r : r + SUB, :] = re * c - im * s
                out[rows + r : rows + r + SUB, :] = re * s + im * c


def mix(parts, woven, table):
    work = sum(part.size for part in parts)
    mixed = pl.pallas_call(
        functools.partial(mix_kernel, woven),
        in_specs=[VMEM_WHOLE] * 5,
        out_shape=[jax.ShapeDtypeStruct(parts[0].shape, jnp.float32)] * 4,
        cost_estimate=pl.CostEstimate(flops=8 * work, bytes_accessed=8 * work, transcendentals=0),
        compiler_params=pltpu.CompilerParams(vmem_limit_bytes=16 << 20),
    )(table, *[parts[m] for m in FAR_FIRST])
    return [mixed[FAR_FIRST.index(m)] for m in range(4)]


def quarter_kernel(start, in_ref, *refs):
    out_refs, sems = refs[:-1], refs[-1]
    quarter = in_ref.shape[1] // len(out_refs)
    group = lax.axis_index("grp")
    copies = []
    for m, out_ref in enumerate(out_refs):
        at = pl.multiple_of((group ^ m) * quarter + start, LANES)
        copies.append(pltpu.make_async_copy(in_ref.at[:, pl.ds(at, out_ref.shape[1])], out_ref, sems.at[m]))
        copies[-1].start()
    for copy in copies:
        copy.wait()


def quarters(series, start, size):
    parts = pl.pallas_call(
        functools.partial(quarter_kernel, start),
        in_specs=[pl.BlockSpec(memory_space=pltpu.HBM)],
        out_specs=[VMEM_WHOLE] * 4,
        out_shape=[jax.ShapeDtypeStruct((2, size), jnp.float32)] * 4,
        scratch_shapes=[pltpu.SemaphoreType.DMA((4,))],
        compiler_params=pltpu.CompilerParams(vmem_limit_bytes=8 << 20),
    )(pltpu.with_memory_space_constraint(series, pltpu.HBM))
    return [part.reshape(2, size // LANES, LANES).transpose(1, 0, 2).reshape(-1, LANES) for part in parts]


def swap(parts, shift):
    return [send(part, m << shift) if m else part for m, part in enumerate(parts)]


def send(part, flip):
    return lax.ppermute(part, AXES, [(d, d ^ flip) for d in range(lax.axis_size(AXES))])


def device_digits():
    d = np.arange(32)
    z, yx, core = d // 8, d // 2 % 4, d % 2
    return z, yx, core, yx + 4 * z + 16 * core


def root(product, modulus):
    c, s = roots(product, modulus)
    return c + 1j * s


def rows_of(columns):
    flat = [columns[0].real] + [part for column in columns[1:] for part in (column.real, column.imag)]
    table = np.zeros((32, LANES), np.float32)
    table[:, : len(flat)] = np.stack(flat, 1)
    return table


def mix_table(mine, digit, factors):
    columns = [root((mine ^ 2) * digit - mine * digit, 4)]
    columns += [root(((mine ^ 1) - mine) * (digit ^ m), 4) for m in range(2)]
    return rows_of(columns + [f * root(mine * (digit ^ m), 4) for block in factors for m, f in enumerate(block)])


def mix_tables(points, start, rows):
    z, yx, core, _ = device_digits()
    first = [[root((2 * yx + core) * (yx ^ m), 32) / math.sqrt(points) for m in range(4)]]
    second = [
        [root(core * (z ^ m), 8) * root((yx + 4 * (z ^ m)) * (z * 8 + start // 32 + b), 1024) for m in range(4)]
        for b in range(rows // 32)
    ]
    return mix_table(z, yx, first), mix_table(yx, z, second)


def slab_kernel(starts, bit_ref, near_ref, mid_ref, turn_ref, fh_ref, fl_ref, *refs):
    in_refs, (out_ref, whole, first, second) = refs[:-4], refs[-4:]
    place = own_place()
    group, pair, core = place // 8, place // 2 % 4, place % 2
    digit = pair + 4 * group + 16 * core
    row = bit_ref[pl.ds(place, 1), :]
    sign = spread(row, 0)
    span, block = 1024, 0
    for h, start in enumerate(starts):
        for m in range(4):
            mine, other = in_refs[h * 8 + FAR_FIRST.index(m)], in_refs[h * 8 + 4 + FAR_FIRST.index(m)]
            rows = mine.shape[0] // 2
            at = pl.multiple_of((group ^ m) * (span // 4) + start, 32)
            for b in range(0, rows, 32):
                c, s = spread(row, 1 + 2 * block), spread(row, 2 + 2 * block)
                block += 1
                for r in range(b, b + 32, SUB):
                    re = other[r : r + SUB, :] + mine[r : r + SUB, :] * sign
                    im = other[rows + r : rows + r + SUB, :] + mine[rows + r : rows + r + SUB, :] * sign
                    whole[pl.ds(at + r, SUB), :] = re * c - im * s
                    whole[pl.ds(span + at + r, SUB), :] = re * s + im * c
    outer = inner = 32
    fold, pitch = outer // SUB, first_pitch(outer, inner)
    for j in range(0, inner, SUB):
        values = []
        for e in range(outer):
            base = e * inner + j
            values.append((whole[base : base + SUB, :], whole[span + base : span + base + SUB, :]))
        at = pl.multiple_of(digit * 2 * inner + j, SUB)
        nc, ns = near_ref[pl.ds(at, SUB), :], near_ref[pl.ds(at + inner, SUB), :]
        for k, (re, im) in enumerate(dft_list(values)):
            base = k * inner + j
            mc, ms = mid_ref[base : base + SUB, :], mid_ref[span + base : span + base + SUB, :]
            c, s = mc * nc - ms * ns, mc * ns + ms * nc
            at = k // fold * pitch + k % fold * inner + j
            first[at : at + SUB, :] = re * c - im * s
            first[SUB * pitch + at : SUB * pitch + at + SUB, :] = re * s + im * c
    lane_stage(outer, inner, turn_ref, fh_ref, fl_ref, out_ref, first, second)


def slab_transform(arrived, lane_rows, points):
    z, _, core, _ = device_digits()
    nc, ns = roots(np.arange(32)[:, None] * np.arange(32 * LANES)[None, :], points)
    near = np.stack([nc, ns], 1).reshape(32 * 2 * 32, LANES).astype(np.float32)
    mid, turn, fh, fl, _ = local_tables(32, 32, lane_rows)
    starts = [sum(CHUNKS[:h]) for h in range(len(CHUNKS))]
    bits = [1 - 2 * core + 0j]
    for start, rows in zip(starts, CHUNKS):
        for m in range(4):
            bits += [root(core * ((z ^ m) * 8 + start // 32 + b), 64) for b in range(rows // 32)]
    return pl.pallas_call(
        functools.partial(slab_kernel, starts),
        in_specs=[VMEM_WHOLE] * (6 + len(arrived)),
        out_shape=jax.ShapeDtypeStruct((32, 64, LANES), jnp.float32),
        scratch_shapes=[
            pltpu.VMEM((2048, LANES), jnp.float32),
            pltpu.VMEM((2 * SUB * first_pitch(32, 32), LANES), jnp.float32),
            pltpu.VMEM((1024, 2 * LANES), jnp.float32),
        ],
        compiler_params=pltpu.CompilerParams(vmem_limit_bytes=20 << 20),
    )(rows_of(bits), near, mid, turn, fh, fl, *arrived)


CHUNKS = (128, 128)


def after(arrays, result):
    return list(lax.optimization_barrier((*arrays, result)))[:-1]


def by_axes(series, points):
    slab = series.shape[1]
    starts = [sum(CHUNKS[:h]) for h in range(len(CHUNKS))]
    tables = [mix_tables(points, start, rows) for start, rows in zip(starts, CHUNKS)]
    one, two = [quarters(series, start * LANES, rows * LANES) for start, rows in zip(starts, CHUNKS)]
    one = swap(one, 3)
    two = swap(two, 3)
    one = after(one, two[1])
    one = mix(one, (True,), tables[0][0])
    one = swap(one, 1)
    one = after(one, two[2])
    one = mix(one, (False,) * (CHUNKS[0] // 32), tables[0][1])
    one = swap(one, 3)
    two = mix(two, (True,), tables[1][0])
    two = swap(two, 1)
    two = mix(two, (False,) * (CHUNKS[1] // 32), tables[1][1])
    two = swap(two, 3)
    arrived = []
    one = after(one[:2], one[2]) + one[2:]
    for parts in (one, two):
        mine = [parts[m] for m in FAR_FIRST]
        arrived += mine + [send(part, 1) for part in mine]
    at = np.arange(32).reshape(8, 4).T.reshape(-1)
    dest, c, low = np.meshgrid(np.argsort(at), np.arange(2), np.arange(4), indexing="ij")
    lane_rows = ((dest * 4 + low).reshape(-1), (c == 1).reshape(-1))
    spectrum = slab_transform(arrived, lane_rows, points)
    landed = lax.all_to_all(spectrum, ORDER, split_axis=0, concat_axis=0, tiled=True).reshape(2048, LANES)
    ordered = order_rows(landed, at[np.argsort(device_digits()[3])].tolist())
    return ordered.reshape(slab // LANES, 2, LANES).transpose(1, 0, 2).reshape(2, slab)


def exchange(blocks, count):
    shape = blocks.shape
    blocks = blocks.reshape((count, shape[0] // count) + shape[1:])
    return lax.all_to_all(blocks, ORDER, split_axis=0, concat_axis=0, tiled=True).reshape(shape)


def local(series):
    count = lax.axis_size("grp") * lax.axis_size("dev")
    slab = series.shape[1]
    points = slab * count
    piece_rows = slab // count // LANES
    if (lax.axis_size("grp"), lax.axis_size("dev"), slab) == (4, 8, 1024 * LANES):
        return by_axes(series, points)
    at = np.arange(count).reshape(lax.axis_size("dev"), lax.axis_size("grp")).T.reshape(-1)
    owners = np.argsort(at)
    tiles = series.reshape(2, count, piece_rows, LANES).transpose(1, 2, 0, 3)
    received = exchange(tiles, count).reshape(2 * slab // LANES, LANES)
    turned = across(received, at.tolist(), points, 1.0 / math.sqrt(points))
    arrived = exchange(turned, count)
    if 2 * LANES == SUB * count:
        lows = LANES // count
        dest, c, low = np.meshgrid(owners, np.arange(2), np.arange(lows), indexing="ij")
        lane_rows = ((dest * lows + low).reshape(-1), (c == 1).reshape(-1))
        spectrum, _ = local_transform(arrived, count, piece_rows, lane_rows)
        landed = exchange(spectrum.reshape(turned.shape), count)
        ordered = order_rows(landed, list(range(count)))
        return ordered.reshape(slab // LANES, 2, LANES).transpose(1, 0, 2).reshape(2, slab)
    freq, c = np.meshgrid(np.arange(LANES), np.arange(2), indexing="ij")
    spectrum, kept = local_transform(arrived, count, piece_rows, (freq.reshape(-1), (c == 1).reshape(-1)))
    spectrum = spectrum.reshape(2 * LANES // SUB, -1, SUB, LANES).transpose(0, 2, 1, 3).reshape(2 * LANES, -1)
    natural = jnp.take(spectrum, np.argsort(kept), axis=1).reshape(LANES, 2, -1)
    blocks = natural.transpose(0, 2, 1).reshape(count, -1, 2)[owners]
    landed = exchange(blocks, count)
    return landed.transpose(2, 1, 0).reshape(2, slab)


def solution(mesh):
    return jax.shard_map(
        local,
        mesh=mesh,
        in_specs=(P(None, AXES),),
        out_specs=P(None, AXES),
        check_vma=False,
    )
```

```python
import functools
import math

import jax
import jax.numpy as jnp
import numpy as np
from jax import lax
from jax.experimental import pallas as pl
from jax.experimental.pallas import tpu as pltpu
from jax.sharding import PartitionSpec as P

LANES = 128
SUB = 8
AXES = ("grp", "dev")
ORDER = ("dev", "grp")


def roots(product, modulus):
    angle = np.asarray(product, np.int64) % modulus * (-2.0 * math.pi / modulus)
    return np.cos(angle), np.sin(angle)


def times_root(value, k, n):
    re, im = value
    k %= n
    if k == 0:
        return value
    if 4 * k == n:
        return im, -re
    if 2 * k == n:
        return -re, -im
    if 4 * k == 3 * n:
        return -im, re
    if 8 * k == n:
        half = np.float32(math.sqrt(0.5))
        return (re + im) * half, (im - re) * half
    if 8 * k == 3 * n:
        half = np.float32(math.sqrt(0.5))
        return (im - re) * half, (re + im) * -half
    angle = -2.0 * math.pi * k / n
    c, s = np.float32(math.cos(angle)), np.float32(math.sin(angle))
    return re * c - im * s, re * s + im * c


def dft_list(values):
    n = len(values)
    if n == 1:
        return values
    even, odd = dft_list(values[0::2]), dft_list(values[1::2])
    low, high = [], []
    for k in range(n // 2):
        (er, ei), (tr, ti) = even[k], times_root(odd[k], k, n)
        low.append((er + tr, ei + ti))
        high.append((er - tr, ei - ti))
    return low + high


def across_kernel(sources, place_ref, turn_ref, step_ref, in_ref, out_ref):
    count = len(sources)
    rows = in_ref.shape[0] // count // 2
    for j in range(0, rows, SUB):
        take = min(SUB, rows - j)
        values = []
        for at in sources:
            base = (at * rows + j) * 2
            values.append((in_ref[pl.ds(base, take, 2), :], in_ref[pl.ds(base + 1, take, 2), :]))
        for k, (re, im) in enumerate(dft_list(values)):
            base = k * 2 * rows + j
            tc, ts = turn_ref[base : base + take, :], turn_ref[base + rows : base + rows + take, :]
            dc, ds = step_ref[0, 2 * k], step_ref[0, 2 * k + 1]
            c, s = tc * dc - ts * ds, tc * ds + ts * dc
            out_ref[base : base + take, :] = re * c - im * s
            out_ref[base + rows : base + rows + take, :] = re * s + im * c


def across(received, sources, points, scale):
    count = len(sources)
    slab = points // count
    piece = slab // count
    digits = np.arange(count)
    tc, ts = roots(digits[:, None] * np.arange(piece)[None, :], points)
    turn = np.stack([tc, ts], 1).reshape(count * 2 * piece // LANES, LANES) * scale
    dc, ds = roots(digits[:, None] * digits[None, :], count * count)
    step = np.stack([dc, ds], 2).reshape(count, 1, 2 * count)
    place = lax.axis_index(ORDER).astype(jnp.int32).reshape(1)
    whole = pl.BlockSpec(received.shape, lambda i, place: (0, 0))
    return pl.pallas_call(
        functools.partial(across_kernel, sources),
        grid_spec=pltpu.PrefetchScalarGridSpec(
            num_scalar_prefetch=1,
            grid=(1,),
            in_specs=[
                whole,
                pl.BlockSpec((None, 1, 2 * count), lambda i, place: (place[0], 0, 0), memory_space=pltpu.SMEM),
                whole,
            ],
            out_specs=whole,
        ),
        out_shape=jax.ShapeDtypeStruct(received.shape, jnp.float32),
        compiler_params=pltpu.CompilerParams(vmem_limit_bytes=32 << 20),
    )(place, turn.astype(np.float32), step.astype(np.float32), received)


def split_bf16(values):
    high = values.astype(jnp.bfloat16)
    return high, (values - high.astype(jnp.float32)).astype(jnp.bfloat16)


def first_pitch(outer, inner):
    return outer // SUB * inner + SUB


def lane_stage(outer, inner, turn_ref, fh_ref, fl_ref, out_ref, first, second):
    span = outer * inner
    fold, pitch = outer // SUB, first_pitch(outer, inner)
    together = max(1, LANES // (inner * SUB))
    dot = functools.partial(
        lax.dot_general, dimension_numbers=(((1,), (1,)), ((), ())), preferred_element_type=jnp.float32
    )
    for begin in range(0, fold, together):
        for v in range(begin, begin + together):
            values = []
            for j in range(inner):
                at = v * inner + j
                values.append((first[pl.ds(at, SUB, pitch), :], first[pl.ds(SUB * pitch + at, SUB, pitch), :]))
            for k, (re, im) in enumerate(dft_list(values)):
                base = (v * inner + k) * SUB
                c, s = turn_ref[base : base + SUB, :], turn_ref[span + base : span + base + SUB, :]
                second[base : base + SUB, :LANES] = re * c - im * s
                second[base : base + SUB, LANES:] = re * s + im * c
        columns = together * inner * SUB
        done = begin * inner * SUB
        xh, xl = split_bf16(second[done : done + columns, :])
        result = dot(fh_ref[...], xh) + (dot(fh_ref[...], xl) + dot(fl_ref[...], xh))
        for t in range(columns // LANES):
            tile = result[:, t * LANES : (t + 1) * LANES]
            at = (done // LANES + t) * SUB
            out_ref[:, at : at + SUB, :] = tile.reshape(tile.shape[0] // SUB, SUB, LANES)


def local_kernel(piece_rows, mid_ref, turn_ref, fh_ref, fl_ref, in_ref, out_ref, first, second):
    inner = piece_rows
    outer = in_ref.shape[0] // 2 // inner
    span = outer * inner
    fold, pitch = outer // SUB, first_pitch(outer, inner)
    for j in range(0, inner, SUB):
        take = min(SUB, inner - j)
        values = []
        for e in range(outer):
            base = e * 2 * inner + j
            values.append((in_ref[base : base + take, :], in_ref[base + inner : base + inner + take, :]))
        for k, (re, im) in enumerate(dft_list(values)):
            base = k * inner + j
            c, s = mid_ref[base : base + take, :], mid_ref[span + base : span + base + take, :]
            at = k // fold * pitch + k % fold * inner + j
            first[at : at + take, :] = re * c - im * s
            first[SUB * pitch + at : SUB * pitch + at + take, :] = re * s + im * c
    lane_stage(outer, inner, turn_ref, fh_ref, fl_ref, out_ref, first, second)


def local_tables(outer, inner, lane_rows):
    span = outer * inner
    slab = span * LANES
    mc, ms = roots(np.arange(outer)[:, None] * np.arange(inner)[None, :], span)
    mid = np.broadcast_to(np.stack([mc, ms]).reshape(2 * span, 1), (2 * span, LANES))
    fold = outer // SUB
    v, k, i = np.meshgrid(np.arange(fold), np.arange(inner), np.arange(SUB), indexing="ij")
    kept = ((v + fold * i) + outer * k).reshape(span)
    tc, ts = roots(kept[:, None] * np.arange(LANES)[None, :], slab)
    turn = np.concatenate([tc, ts])
    freq, imag = lane_rows
    fc, fs = roots(freq[:, None] * np.arange(LANES)[None, :], LANES)
    lane = np.where(imag[:, None], np.concatenate([fs, fc], 1), np.concatenate([fc, -fs], 1)).astype(np.float32)
    fh = lane.astype(jnp.bfloat16)
    fl = (lane - fh.astype(np.float32)).astype(jnp.bfloat16)
    return mid.astype(np.float32), turn.astype(np.float32), fh, fl, kept


def local_transform(arrived, outer, inner, lane_rows):
    span = outer * inner
    mid, turn, fh, fl, kept = local_tables(outer, inner, lane_rows)
    return pl.pallas_call(
        functools.partial(local_kernel, inner),
        out_shape=jax.ShapeDtypeStruct((2 * LANES // SUB, SUB * span // LANES, LANES), jnp.float32),
        scratch_shapes=[
            pltpu.VMEM((2 * SUB * first_pitch(outer, inner), LANES), jnp.float32),
            pltpu.VMEM((span, 2 * LANES), jnp.float32),
        ],
        compiler_params=pltpu.CompilerParams(vmem_limit_bytes=20 << 20),
    )(mid, turn, fh, fl, arrived), kept


def order_kernel(sources, in_ref, out_ref, whole, ordered, sems):
    count = len(sources)
    fold = LANES // count
    each = in_ref.shape[0] // count
    tiles = each // SUB // fold
    lows = SUB // 2
    rows = tiles * LANES * 2
    pitch = each + SUB
    for k, at in enumerate(sources):
        whole[k * pitch : k * pitch + each, :] = in_ref[at * each : (at + 1) * each, :]
    copies = []
    for low in range(lows):
        for t in range(tiles):
            base = low * rows + t * LANES * 2
            for c in range(2):
                parts = [
                    whole[pl.ds((v * tiles + t) * SUB + c * lows + low, count, pitch), :] for v in range(fold)
                ]
                ordered[pl.ds(base + c, LANES, 2), :] = jnp.concatenate(parts, 0).T
            piece = pl.ds(base, LANES * 2)
            copies.append(pltpu.make_async_copy(ordered.at[piece, :], out_ref.at[piece, :], sems.at[low, t]))
            copies[-1].start()
    for copy in copies:
        copy.wait()


def order_rows(landed, sources):
    return pl.pallas_call(
        functools.partial(order_kernel, sources),
        in_specs=[pl.BlockSpec(memory_space=pltpu.VMEM)],
        out_specs=pl.BlockSpec(memory_space=pltpu.HBM),
        out_shape=jax.ShapeDtypeStruct(landed.shape, jnp.float32),
        scratch_shapes=[
            pltpu.VMEM((landed.shape[0] + SUB * len(sources), LANES), jnp.float32),
            pltpu.VMEM(landed.shape, jnp.float32),
            pltpu.SemaphoreType.DMA((SUB // 2, landed.shape[0] // SUB // LANES)),
        ],
        compiler_params=pltpu.CompilerParams(vmem_limit_bytes=16 << 20),
    )(landed)


VMEM_WHOLE = pl.BlockSpec(memory_space=pltpu.VMEM)
FAR_FIRST = (0, 2, 3, 1)


def own_place():
    return lax.axis_index("grp") * 8 + lax.axis_index("dev")


def spread(row, at):
    return jnp.broadcast_to(row[:, at : at + 1], (SUB, LANES))


def mix_kernel(woven, coef_ref, *refs):
    ins, outs = [None] * 4, [None] * 4
    for n, m in enumerate(FAR_FIRST):
        ins[m], outs[m] = refs[n], refs[4 + n]
    rows = refs[0].shape[0] // 2
    row = coef_ref[pl.ds(own_place(), 1), :]
    parity = spread(row, 0)
    turns = [(spread(row, 1 + 2 * m), spread(row, 2 + 2 * m)) for m in range(2)]
    blocks = len(woven)
    for b in range(blocks):
        factors = [(spread(row, 5 + 8 * b + 2 * m), spread(row, 6 + 8 * b + 2 * m)) for m in range(4)]
        for r in range(b * rows // blocks, (b + 1) * rows // blocks, SUB):
            if woven[b]:
                values = [(ref[pl.ds(2 * r, SUB, 2), :], ref[pl.ds(2 * r + 1, SUB, 2), :]) for ref in ins]
            else:
                values = [(ref[r : r + SUB, :], ref[rows + r : rows + r + SUB, :]) for ref in ins]
            (r0, i0), (r1, i1), (r2, i2), (r3, i3) = values
            r2, i2, r3, i3 = r2 * parity, i2 * parity, r3 * parity, i3 * parity
            results = [None] * 4
            for m, (pr, pi, qr, qi) in enumerate(
                ((r0 + r2, i0 + i2, r1 + r3, i1 + i3), (r0 - r2, i0 - i2, r1 - r3, i1 - i3))
            ):
                tc, ts = turns[m]
                tr, ti = qr * tc - qi * ts, qr * ts + qi * tc
                results[m], results[m + 2] = (pr + tr, pi + ti), (pr - tr, pi - ti)
            for out, (re, im), (c, s) in zip(outs, results, factors):
                out[r : r + SUB, :] = re * c - im * s
                out[rows + r : rows + r + SUB, :] = re * s + im * c


def mix(parts, woven, table):
    work = sum(part.size for part in parts)
    mixed = pl.pallas_call(
        functools.partial(mix_kernel, woven),
        in_specs=[VMEM_WHOLE] * 5,
        out_shape=[jax.ShapeDtypeStruct(parts[0].shape, jnp.float32)] * 4,
        cost_estimate=pl.CostEstimate(flops=8 * work, bytes_accessed=8 * work, transcendentals=0),
        compiler_params=pltpu.CompilerParams(vmem_limit_bytes=16 << 20),
    )(table, *[parts[m] for m in FAR_FIRST])
    return [mixed[FAR_FIRST.index(m)] for m in range(4)]


def quarter_kernel(start, in_ref, *refs):
    out_refs, sems = refs[:-1], refs[-1]
    quarter = in_ref.shape[1] // len(out_refs)
    group = lax.axis_index("grp")
    copies = []
    for m, out_ref in enumerate(out_refs):
        at = pl.multiple_of((group ^ m) * quarter + start, LANES)
        copies.append(pltpu.make_async_copy(in_ref.at[:, pl.ds(at, out_ref.shape[1])], out_ref, sems.at[m]))
        copies[-1].start()
    for copy in copies:
        copy.wait()


def quarters(series, start, size):
    parts = pl.pallas_call(
        functools.partial(quarter_kernel, start),
        in_specs=[pl.BlockSpec(memory_space=pltpu.HBM)],
        out_specs=[VMEM_WHOLE] * 4,
        out_shape=[jax.ShapeDtypeStruct((2, size), jnp.float32)] * 4,
        scratch_shapes=[pltpu.SemaphoreType.DMA((4,))],
        compiler_params=pltpu.CompilerParams(vmem_limit_bytes=8 << 20),
    )(pltpu.with_memory_space_constraint(series, pltpu.HBM))
    return [part.reshape(2, size // LANES, LANES).transpose(1, 0, 2).reshape(-1, LANES) for part in parts]


def swap(parts, shift):
    return [send(part, m << shift) if m else part for m, part in enumerate(parts)]


def send(part, flip):
    return lax.ppermute(part, AXES, [(d, d ^ flip) for d in range(lax.axis_size(AXES))])


def device_digits():
    d = np.arange(32)
    z, yx, core = d // 8, d // 2 % 4, d % 2
    return z, yx, core, yx + 4 * z + 16 * core


def root(product, modulus):
    c, s = roots(product, modulus)
    return c + 1j * s


def rows_of(columns):
    flat = [columns[0].real] + [part for column in columns[1:] for part in (column.real, column.imag)]
    table = np.zeros((32, LANES), np.float32)
    table[:, : len(flat)] = np.stack(flat, 1)
    return table


def mix_table(mine, digit, factors):
    columns = [root((mine ^ 2) * digit - mine * digit, 4)]
    columns += [root(((mine ^ 1) - mine) * (digit ^ m), 4) for m in range(2)]
    return rows_of(columns + [f * root(mine * (digit ^ m), 4) for block in factors for m, f in enumerate(block)])


def mix_tables(points, start, rows):
    z, yx, core, _ = device_digits()
    first = [[root((2 * yx + core) * (yx ^ m), 32) / math.sqrt(points) for m in range(4)]]
    second = [
        [root(core * (z ^ m), 8) * root((yx + 4 * (z ^ m)) * (z * 8 + start // 32 + b), 1024) for m in range(4)]
        for b in range(rows // 32)
    ]
    return mix_table(z, yx, first), mix_table(yx, z, second)


def slab_kernel(starts, bit_ref, near_ref, mid_ref, turn_ref, fh_ref, fl_ref, *refs):
    in_refs, (out_ref, whole, first, second) = refs[:-4], refs[-4:]
    place = own_place()
    group, pair, core = place // 8, place // 2 % 4, place % 2
    digit = pair + 4 * group + 16 * core
    row = bit_ref[pl.ds(place, 1), :]
    sign = spread(row, 0)
    span, block = 1024, 0
    for h, start in enumerate(starts):
        for m in range(4):
            mine, other = in_refs[h * 8 + FAR_FIRST.index(m)], in_refs[h * 8 + 4 + FAR_FIRST.index(m)]
            rows = mine.shape[0] // 2
            at = pl.multiple_of((group ^ m) * (span // 4) + start, 32)
            for b in range(0, rows, 32):
                c, s = spread(row, 1 + 2 * block), spread(row, 2 + 2 * block)
                block += 1
                for r in range(b, b + 32, SUB):
                    re = other[r : r + SUB, :] + mine[r : r + SUB, :] * sign
                    im = other[rows + r : rows + r + SUB, :] + mine[rows + r : rows + r + SUB, :] * sign
                    whole[pl.ds(at + r, SUB), :] = re * c - im * s
                    whole[pl.ds(span + at + r, SUB), :] = re * s + im * c
    outer = inner = 32
    fold, pitch = outer // SUB, first_pitch(outer, inner)
    for j in range(0, inner, SUB):
        values = []
        for e in range(outer):
            base = e * inner + j
            values.append((whole[base : base + SUB, :], whole[span + base : span + base + SUB, :]))
        at = pl.multiple_of(digit * 2 * inner + j, SUB)
        nc, ns = near_ref[pl.ds(at, SUB), :], near_ref[pl.ds(at + inner, SUB), :]
        for k, (re, im) in enumerate(dft_list(values)):
            base = k * inner + j
            mc, ms = mid_ref[base : base + SUB, :], mid_ref[span + base : span + base + SUB, :]
            c, s = mc * nc - ms * ns, mc * ns + ms * nc
            at = k // fold * pitch + k % fold * inner + j
            first[at : at + SUB, :] = re * c - im * s
            first[SUB * pitch + at : SUB * pitch + at + SUB, :] = re * s + im * c
    lane_stage(outer, inner, turn_ref, fh_ref, fl_ref, out_ref, first, second)


def slab_transform(arrived, lane_rows, points):
    z, _, core, _ = device_digits()
    nc, ns = roots(np.arange(32)[:, None] * np.arange(32 * LANES)[None, :], points)
    near = np.stack([nc, ns], 1).reshape(32 * 2 * 32, LANES).astype(np.float32)
    mid, turn, fh, fl, _ = local_tables(32, 32, lane_rows)
    starts = [sum(CHUNKS[:h]) for h in range(len(CHUNKS))]
    bits = [1 - 2 * core + 0j]
    for start, rows in zip(starts, CHUNKS):
        for m in range(4):
            bits += [root(core * ((z ^ m) * 8 + start // 32 + b), 64) for b in range(rows // 32)]
    return pl.pallas_call(
        functools.partial(slab_kernel, starts),
        in_specs=[VMEM_WHOLE] * (6 + len(arrived)),
        out_shape=jax.ShapeDtypeStruct((32, 64, LANES), jnp.float32),
        scratch_shapes=[
            pltpu.VMEM((2048, LANES), jnp.float32),
            pltpu.VMEM((2 * SUB * first_pitch(32, 32), LANES), jnp.float32),
            pltpu.VMEM((1024, 2 * LANES), jnp.float32),
        ],
        compiler_params=pltpu.CompilerParams(vmem_limit_bytes=20 << 20),
    )(rows_of(bits), near, mid, turn, fh, fl, *arrived)


CHUNKS = (128, 128)


def after(arrays, result):
    return list(lax.optimization_barrier((*arrays, result)))[:-1]


def by_axes(series, points):
    slab = series.shape[1]
    starts = [sum(CHUNKS[:h]) for h in range(len(CHUNKS))]
    tables = [mix_tables(points, start, rows) for start, rows in zip(starts, CHUNKS)]
    one, two = [quarters(series, start * LANES, rows * LANES) for start, rows in zip(starts, CHUNKS)]
    one = swap(one, 3)
    two = swap(two, 3)
    one = after(one, two[1])
    one = mix(one, (True,), tables[0][0])
    one = swap(one, 1)
    one = after(one, two[2])
    one = mix(one, (False,) * (CHUNKS[0] // 32), tables[0][1])
    one = swap(one, 3)
    two = mix(two, (True,), tables[1][0])
    two = swap(two, 1)
    two = mix(two, (False,) * (CHUNKS[1] // 32), tables[1][1])
    two = swap(two, 3)
    arrived = []
    one = after(one[:2], one[2]) + one[2:]
    for parts in (one, two):
        mine = [parts[m] for m in FAR_FIRST]
        arrived += mine + [send(part, 1) for part in mine]
    dest, c, low = np.meshgrid(np.arange(32), np.arange(2), np.arange(4), indexing="ij")
    lane_rows = ((dest * 4 + low).reshape(-1), (c == 1).reshape(-1))
    spectrum = slab_transform(arrived, lane_rows, points)
    landed = lax.all_to_all(spectrum, AXES, split_axis=0, concat_axis=0, tiled=True).reshape(2048, LANES)
    ordered = order_rows(landed, np.argsort(device_digits()[3]).tolist())
    return ordered.reshape(slab // LANES, 2, LANES).transpose(1, 0, 2).reshape(2, slab)


def exchange(blocks, count):
    shape = blocks.shape
    blocks = blocks.reshape((count, shape[0] // count) + shape[1:])
    return lax.all_to_all(blocks, ORDER, split_axis=0, concat_axis=0, tiled=True).reshape(shape)


def local(series):
    count = lax.axis_size("grp") * lax.axis_size("dev")
    slab = series.shape[1]
    points = slab * count
    piece_rows = slab // count // LANES
    if (lax.axis_size("grp"), lax.axis_size("dev"), slab) == (4, 8, 1024 * LANES):
        return by_axes(series, points)
    at = np.arange(count).reshape(lax.axis_size("dev"), lax.axis_size("grp")).T.reshape(-1)
    owners = np.argsort(at)
    tiles = series.reshape(2, count, piece_rows, LANES).transpose(1, 2, 0, 3)
    received = exchange(tiles, count).reshape(2 * slab // LANES, LANES)
    turned = across(received, at.tolist(), points, 1.0 / math.sqrt(points))
    arrived = exchange(turned, count)
    if 2 * LANES == SUB * count:
        lows = LANES // count
        dest, c, low = np.meshgrid(owners, np.arange(2), np.arange(lows), indexing="ij")
        lane_rows = ((dest * lows + low).reshape(-1), (c == 1).reshape(-1))
        spectrum, _ = local_transform(arrived, count, piece_rows, lane_rows)
        landed = exchange(spectrum.reshape(turned.shape), count)
        ordered = order_rows(landed, list(range(count)))
        return ordered.reshape(slab // LANES, 2, LANES).transpose(1, 0, 2).reshape(2, slab)
    freq, c = np.meshgrid(np.arange(LANES), np.arange(2), indexing="ij")
    spectrum, kept = local_transform(arrived, count, piece_rows, (freq.reshape(-1), (c == 1).reshape(-1)))
    spectrum = spectrum.reshape(2 * LANES // SUB, -1, SUB, LANES).transpose(0, 2, 1, 3).reshape(2 * LANES, -1)
    natural = jnp.take(spectrum, np.argsort(kept), axis=1).reshape(LANES, 2, -1)
    blocks = natural.transpose(0, 2, 1).reshape(count, -1, 2)[owners]
    landed = exchange(blocks, count)
    return landed.transpose(2, 1, 0).reshape(2, slab)


def solution(mesh):
    return jax.shard_map(
        local,
        mesh=mesh,
        in_specs=(P(None, AXES),),
        out_specs=P(None, AXES),
        check_vma=False,
    )
```
